256 devices in a mesh: lat: 8 (over z), lon: 32 (over x, y, core).
Axes of the slice: x: 4, y: 4, z: 8, core: 2. Of those that a mesh axis runs over, the one named last changes fastest.
Arguments:
- thickness: float32 [16, 512, 11520], P(None, 'lat', 'lon'), may hold values from 0.5 to 1.5
- wind: float32 [2, 16, 512, 11520], P(None, None, 'lat', 'lon'), may hold values from -6 to 6
- cutoff: int32 [256], replicated, may hold values from 1 to 2880, as said below
Outputs:
- thick_out: float32 [16, 512, 11520], P(None, 'lat', 'lon')
- wind_out: float32 [2, 16, 512, 11520], P(None, None, 'lat', 'lon')
The draws below stay inside these ranges and needn't reach their ends.
Inputs may be any that keep to these rules, and one draw needn't show every extreme that they name: `cutoff`: some row keeps exactly 2880 and some row exactly 1.
All inputs are finite; a program needn't handle non-finite values.
Results may differ from the reference program's by a relative error of at most 0.000075.
Values sent between devices are 32-bit elements; how exact they have to be, the bound alone decides.
A program may use at most 128 MiB of HBM per device.

```python
import jax
import jax.numpy as jnp
from jax import lax

LEV = 16
NLAT = 512
NLON = 11520
NPOLAR = 256
KMAX = 2880


def draw_cutoff(key, part):
    key = jax.random.fold_in(key, 7)
    key_vals, key_top, key_low = jax.random.split(key, 3)
    values = jax.random.randint(key_vals, (NPOLAR,), 1, KMAX + 1)
    top_row = jax.random.randint(key_top, (), 0, NPOLAR)
    low_row = (top_row + 1 + jax.random.randint(key_low, (), 0, NPOLAR - 1)) % NPOLAR
    places = jnp.arange(NPOLAR)
    values = jnp.where(places == top_row, KMAX, values)
    values = jnp.where(places == low_row, 1, values)
    return values.astype(jnp.int32)


def level_of(rng, extent, pieces, least, high):
    loudness = 1.0
    for position, shards_of in pieces:
        steps = jax.random.uniform(jax.random.fold_in(jax.random.fold_in(rng, 6), position), (shards_of,), jnp.float32, least / len(pieces), high / len(pieces))
        loudness = loudness * jnp.repeat(jnp.exp(steps), extent[position] // shards_of).reshape((-1,) + (1,) * (len(extent) - 1 - position))
    return loudness


def noise(rng, shape, scale, reach, cuts=(), kind=jnp.bfloat16):
    loudness = level_of(rng, shape, cuts, -0.22, 0.18) if cuts else 1.0
    result = jax.random.normal(rng, shape, jnp.float32) * scale * loudness
    return jnp.minimum(jnp.maximum(result, -reach), reach).astype(kind)


def setup_inputs(seed: int = 0) -> dict:
    key_list = jax.random.split(jax.random.key(seed), 4)
    return {
        "thickness": jnp.clip(0.5 + 1.0 * jax.random.uniform(key_list[0], (LEV, NLAT, NLON), jnp.float32) ** level_of(key_list[0], (LEV, NLAT, NLON), ((1, 8), (2, 32)), -0.2, 0.2), 0.5, 1.5),
        "wind": noise(key_list[1], (2, LEV, NLAT, NLON), 1.0, 6.0, ((2, 8), (3, 32)), jnp.float32),
        "cutoff": draw_cutoff(jax.random.fold_in(key_list[3], 71), 0),
    }


advect_coef = 0.05
press_coef = 0.1


def reference(thickness, wind, cutoff):
    row_index = jnp.arange(NLAT).astype(jnp.float32)
    latitude = jnp.pi * ((row_index + 0.5) / NLAT - 0.5)
    cosine = jnp.cos(latitude)
    metric = 1.0 / jnp.maximum(cosine, 0.2)
    cosine_col = cosine[:, None]
    metric_col = metric[:, None]
    east_wind = wind[0]
    north_wind = wind[1]
    flux_lon = thickness * east_wind
    flux_lat = thickness * north_wind * cosine_col
    lon_diff = jnp.roll(flux_lon, -1, axis=2) - jnp.roll(flux_lon, 1, axis=2)
    padded = jnp.pad(flux_lat, ((0, 0), (1, 1), (0, 0)))
    lat_diff = padded[:, 2:] - padded[:, :-2]
    advected = thickness - advect_coef * metric_col * (lon_diff + lat_diff)
    stacked = jnp.concatenate([advected[None], wind], 0)
    quarter = NLAT // 4
    polar_rows = jnp.concatenate([stacked[:, :, :quarter], stacked[:, :, NLAT - quarter:]], 2)
    waves = jnp.arange(NLON // 2 + 1).astype(jnp.int32)
    retain = waves[None, :] <= cutoff.astype(jnp.int32)[:, None]

    def smooth_field(field):
        spectra = jnp.fft.rfft(field, axis=2)
        spectra = jnp.where(retain[None], spectra, 0)
        return jnp.fft.irfft(spectra, n=NLON, axis=2).astype(field.dtype)

    smoothed = lax.map(smooth_field, polar_rows)
    filtered = jnp.concatenate([smoothed[:, :, :quarter], stacked[:, :, quarter:NLAT - quarter], smoothed[:, :, quarter:]], 2)
    thick_out = filtered[0]
    lon_h = jnp.roll(thick_out, -1, axis=2) - jnp.roll(thick_out, 1, axis=2)
    padded_h = jnp.pad(thick_out, ((0, 0), (1, 1), (0, 0)))
    lat_h = padded_h[:, 2:] - padded_h[:, :-2]
    east_out = filtered[1] - press_coef * metric_col * lon_h
    north_out = filtered[2] - press_coef * lat_h
    return thick_out, jnp.stack([east_out, north_out], 0)
```

```python
import math

import jax
import jax.numpy as jnp
import numpy as np
from jax import lax
from jax.sharding import PartitionSpec as P

advect_coef = 0.05
press_coef = 0.1
RANK = 24


def cauchy_tables(columns, count):
    total = columns * count
    inside = np.arange(columns)
    outside = np.arange(columns, total)
    far = 1.0 / (total * np.sin(np.pi * (inside[:, None] - outside[None]) / total))
    basis = np.linalg.svd(far, full_matrices=False)[0][:, :RANK]
    gap = inside[:, None] - inside[None]
    near = np.where(gap == 0, 0.0, 1.0 / (total * np.sin(np.pi * gap / total) + (gap == 0)))
    cross = np.zeros((count, RANK, count, RANK))
    for shift in range(1 - count, count):
        if shift == 0:
            continue
        piece = basis.T @ (1.0 / (total * np.sin(np.pi * (gap + shift * columns) / total))) @ basis
        for p in range(count):
            q = p - shift
            if 0 <= q < count:
                cross[p, :, q, :] = piece
    return near, basis, cross


def padded(cells, sides, width, closed):
    for axis, dim in sides:
        count = lax.axis_size(axis)
        ends = count if closed else count - 1
        head = lax.slice_in_dim(cells, 0, width, axis=dim)
        tail = lax.slice_in_dim(cells, cells.shape[dim] - width, cells.shape[dim], axis=dim)
        cells = jnp.concatenate(
            [
                lax.ppermute(tail, axis, [(i, (i + 1) % count) for i in range(ends)]),
                cells,
                lax.ppermute(head, axis, [((i + 1) % count, i) for i in range(ends)]),
            ],
            axis=dim,
        )
    return cells


def smooth(block, cuts):
    items, rows, columns = block.shape
    count = lax.axis_size("lon")
    total = columns * count
    near, basis, cross = cauchy_tables(columns, count)
    near = jnp.asarray(near, jnp.float32)
    basis = jnp.asarray(basis, jnp.float32)
    cross = jnp.asarray(cross, jnp.float32)
    high = lax.Precision.HIGH
    column = lax.axis_index("lon") * columns + lax.broadcasted_iota(jnp.int32, (rows, columns), 1)
    odd = (2 * cuts + 1)[:, None]
    angle = (odd * column % (2 * total)).astype(jnp.float32) * (math.pi / total)
    turn = jnp.stack([jnp.cos(angle), jnp.sin(angle)])
    waves = (block[None] * turn[:, None]).reshape(2 * items * rows, columns)
    short = jnp.einsum("nl,lf->nf", waves, basis, precision=high)
    group = items * rows // count
    short = short.reshape(2, count, group, RANK).transpose(1, 0, 2, 3).reshape(count, 2 * group, RANK)
    short = lax.all_to_all(short, "lon", split_axis=0, concat_axis=0, tiled=True)
    local = jnp.einsum("nl,ml->nm", waves, near, precision=high)
    moved = jnp.einsum("qnf,pgqf->png", short, cross, precision=high)
    moved = lax.all_to_all(moved, "lon", split_axis=0, concat_axis=0, tiled=True)
    moved = moved.reshape(count, 2, group, RANK).transpose(1, 0, 2, 3).reshape(2 * items * rows, RANK)
    parts = (local + jnp.einsum("nf,lf->nl", moved, basis, precision=high)).reshape(2, items, rows, columns)
    own = odd.astype(jnp.float32) / total
    return turn[1] * parts[0] - turn[0] * parts[1] + own * block


def edge_cells(lon_field, lat_field):
    lon_ext = padded(lon_field, (("lon", 2),), 1, True)
    lat_ext = padded(lat_field, (("lat", 1),), 1, False)
    return (lon_ext, lat_ext)


def body(thickness, wind, cutoff):
    levels, band_rows, columns = thickness.shape
    lat_count = lax.axis_size("lat")
    lat_index = lax.axis_index("lat")
    full_lat = band_rows * lat_count
    global_rows = lat_index * band_rows + lax.broadcasted_iota(jnp.int32, (band_rows, 1), 0)
    latitude = jnp.pi * ((global_rows.astype(jnp.float32) + 0.5) / full_lat - 0.5)
    cosine = jnp.cos(latitude)
    metric = 1.0 / jnp.maximum(cosine, 0.2)
    east_wind = wind[0]
    north_wind = wind[1]
    flux_lon = thickness * east_wind
    flux_lat = thickness * north_wind * cosine
    lon_ext, lat_ext = edge_cells(flux_lon, flux_lat)
    advected = thickness - advect_coef * metric * (
        lon_ext[:, :, 2:] - lon_ext[:, :, :-2] + (lat_ext[:, 2:] - lat_ext[:, :-2])
    )
    stacked = jnp.concatenate([advected[None], wind], 0).reshape(3 * levels, band_rows, columns)
    quarter = full_lat // 4
    full_cut = jnp.concatenate(
        [
            cutoff[:quarter],
            jnp.zeros((full_lat - 2 * quarter,), jnp.int32),
            cutoff[quarter:],
        ]
    )
    row_cuts = lax.dynamic_slice_in_dim(full_cut, lat_index * band_rows, band_rows)
    polar = (global_rows < quarter) | (global_rows >= full_lat - quarter)
    filtered = jnp.where(polar, smooth(stacked, row_cuts), stacked)
    thick_out = filtered[:levels]
    east_filt = filtered[levels : 2 * levels]
    north_filt = filtered[2 * levels :]
    lon_h, lat_h = edge_cells(thick_out, thick_out)
    east_out = east_filt - press_coef * metric * (lon_h[:, :, 2:] - lon_h[:, :, :-2])
    north_out = north_filt - press_coef * (lat_h[:, 2:] - lat_h[:, :-2])
    return (thick_out, jnp.stack([east_out, north_out], 0))


def solution(mesh):
    in_specs = (P(None, "lat", "lon"), P(None, None, "lat", "lon"), P())
    out_specs = (P(None, "lat", "lon"), P(None, None, "lat", "lon"))
    return jax.shard_map(body, mesh=mesh, in_specs=in_specs, out_specs=out_specs, check_vma=False)
```

```python
import functools
import math

import jax
import jax.numpy as jnp
import numpy as np
from jax import lax
from jax.experimental import pallas as pl
from jax.experimental.pallas import tpu as pltpu
from jax.sharding import PartitionSpec as P

MESH = pl.DeviceIdType.MESH
F32 = jnp.float32
BF16 = jnp.bfloat16

advect_coef = 0.05
press_coef = 0.1
RANK = 24
LEVELS = 16
ROWS = 64
COLS = 360
WIDE = 384
BANDS = 8
RING = 32
TOTAL = COLS * RING
PAIRS = LEVELS // 2
CHUNKS = 3 * PAIRS
ITEMS = 2 * ROWS


def cauchy_tables():
    inside = np.arange(COLS)
    outside = np.arange(COLS, TOTAL)
    far = 1.0 / (TOTAL * np.sin(np.pi * (inside[:, None] - outside[None]) / TOTAL))
    basis = np.linalg.svd(far, full_matrices=False)[0][:, :RANK]
    gap = inside[:, None] - inside[None]
    near = np.where(gap == 0, 0.0, 1.0 / (TOTAL * np.sin(np.pi * gap / TOTAL) + (gap == 0)))
    cross = np.zeros((RING, RANK, RING, RANK))
    for shift in range(1 - RING, RING):
        if shift == 0:
            continue
        piece = basis.T @ (1.0 / (TOTAL * np.sin(np.pi * (gap + shift * COLS) / TOTAL))) @ basis
        for p in range(RING):
            if 0 <= p - shift < RING:
                cross[p, :, p - shift, :] = piece
    return near, basis, cross.reshape(RING * RANK, RING * RANK)


def two_parts(table):
    table = table.astype(np.float32)
    high = table.astype(BF16)
    low = (table - high.astype(np.float32)).astype(BF16)
    return high, low


def split(values):
    high = values.astype(BF16)
    return high, (values - high.astype(F32)).astype(BF16)


def dot(left, right, dims):
    return lax.dot_general(left, right, (dims, ((), ())), preferred_element_type=F32)


def place():
    z = lax.axis_index("lat")
    p = lax.axis_index("lon")
    return z, p


def latitude_tables(z, shape):
    row = lax.broadcasted_iota(jnp.int32, shape, 0) + z * ROWS
    latitude = math.pi * ((row.astype(F32) + 0.5) / (ROWS * BANDS) - 0.5)
    cosine = jnp.cos(latitude)
    return cosine, 1.0 / jnp.maximum(cosine, 0.2)


def worker(phase, q):
    x = q // 2
    y = 2 * (q % 2) + (x + phase % 2) % 2
    return x * 8 + y * 2 + phase // 2


def far_kernel(
    cut_ref, shrink_ref, grow_ref, th_hbm, wind_hbm, near_hbm, cross_hbm,
    ext_hbm, out_hbm,
    th, w, ext, xhi, xlo, turn, geo, wide, near, cross, u, zin, vs, vr, zhi, zlo,
    lon_out, lon_in, lat_out, lat_in,
    load_sem, u_sem, z_sem, v_sem, vr_sem, lon_sem, lonr_sem, lat_sem, latr_sem, done_sem,
):
    z, p = place()
    polar = (z < 2) | (z >= 6)
    loads = [
        pltpu.make_async_copy(wind_hbm.at[0], w.at[0], load_sem.at[0]),
        pltpu.make_async_copy(th_hbm, th, load_sem.at[1]),
        pltpu.make_async_copy(wind_hbm.at[1], w.at[1], load_sem.at[2]),
        pltpu.make_async_copy(near_hbm, near, load_sem.at[3]),
        pltpu.make_async_copy(cross_hbm, cross, load_sem.at[4]),
    ]
    for copy in loads:
        copy.start()
    barrier = pltpu.get_barrier_semaphore()

    def greet(i, carry):
        pl.semaphore_signal(barrier, inc=1, device_id=(z, (p + i) % RING), device_id_type=MESH)
        return carry

    lax.fori_loop(1, RING, greet, 0)
    for dz in (1, BANDS - 1):
        pl.semaphore_signal(barrier, inc=1, device_id=((z + dz) % BANDS, p), device_id_type=MESH)

    cosine, metric = latitude_tables(z, (ROWS, WIDE))
    for half in range(2):
        geo[0, half * ROWS : (half + 1) * ROWS] = cosine
        geo[1, half * ROWS : (half + 1) * ROWS] = advect_coef * metric
    wide[...] = jnp.zeros((ITEMS, WIDE), F32)

    @pl.when(polar)
    def _():
        band = jnp.where(z < 2, z, z - 4)
        row = lax.broadcasted_iota(jnp.int32, (ROWS, 4 * ROWS), 0) + band * ROWS
        lane = lax.broadcasted_iota(jnp.int32, (ROWS, 4 * ROWS), 1)
        cuts = jnp.broadcast_to(cut_ref[...].astype(F32), (ROWS, 4 * ROWS))
        limit = jnp.sum(jnp.where(row == lane, cuts, 0.0), axis=1, keepdims=True)
        odd = 2.0 * limit + 1.0
        column = p * COLS + lax.broadcasted_iota(jnp.int32, (ROWS, WIDE), 1)
        product = jnp.broadcast_to(odd, (ROWS, WIDE)).astype(jnp.int32) * column
        laps = jnp.floor(product.astype(F32) * (0.5 / TOTAL)).astype(jnp.int32)
        angle = (product - laps * (2 * TOTAL)).astype(F32) * (math.pi / TOTAL)
        tables = (jnp.cos(angle), jnp.sin(angle), jnp.broadcast_to(odd * (1.0 / TOTAL), (ROWS, WIDE)))
        for k, table in enumerate(tables):
            for half in range(2):
                turn[k, half * ROWS : (half + 1) * ROWS] = table

        def clear(ch, carry):
            xhi[ch, :, 256:] = jnp.zeros((2 * ITEMS, 128), BF16)
            xlo[ch, :, 256:] = jnp.zeros((2 * ITEMS, 128), BF16)
            return carry

        lax.fori_loop(0, CHUNKS, clear, 0)

    pl.semaphore_wait(barrier, RING + 1)

    lane = lax.broadcasted_iota(jnp.int32, (ITEMS, 128), 1)

    def send_lon(kind, first, last):
        edges = jnp.zeros((ITEMS, 128), F32)
        for i in range(PAIRS):
            edges = jnp.where(lane == i, first(i), edges)
            edges = jnp.where(lane == PAIRS + i, last(i), edges)
        lon_out[kind] = edges
        for side, step in ((0, 1), (1, RING - 1)):
            lon_copy(kind, side, step).start()

    def lon_copy(kind, side, step):
        return pltpu.make_async_remote_copy(
            src_ref=lon_out.at[kind], dst_ref=lon_in.at[kind, side],
            send_sem=lon_sem.at[kind, side], recv_sem=lonr_sem.at[kind, side],
            device_id=(z, (p + step) % RING), device_id_type=MESH,
        )

    def lat_copy(kind, side, step):
        return pltpu.make_async_remote_copy(
            src_ref=lat_out.at[kind, side], dst_ref=lat_in.at[kind, side],
            send_sem=lat_sem.at[kind, side], recv_sem=latr_sem.at[kind, side],
            device_id=((z + step) % BANDS, p), device_id_type=MESH,
        )

    def wait_edges(kind):
        for side, step in ((0, 1), (1, RING - 1)):
            lon_copy(kind, side, step).wait()
        for side, step in ((0, 1), (1, BANDS - 1)):
            lat_copy(kind, side, step).wait()

    def with_edges(kind, i, tile):
        left = lon_in[kind, 0, :, PAIRS + i : PAIRS + i + 1]
        right = lon_in[kind, 1, :, i : i + 1]
        return jnp.where(lane == COLS - 256, right, jnp.where(lane == 127, left, tile))

    loads[0].wait()
    loads[1].wait()

    def flux_first(i):
        return (th[2 * i : 2 * i + 2, :, 0:128] * w[0, 2 * i : 2 * i + 2, :, 0:128]).reshape(ITEMS, 128)[:, 0:1]

    def flux_last(i):
        tile = th[2 * i : 2 * i + 2, :, 256:COLS] * w[0, 2 * i : 2 * i + 2, :, 256:COLS]
        return tile.reshape(ITEMS, COLS - 256)[:, COLS - 257 : COLS - 256]

    send_lon(0, flux_first, flux_last)
    loads[2].wait()
    for side, row in ((0, ROWS - 1), (1, 0)):
        for lev in range(LEVELS):
            lat_out[0, side, lev : lev + 1, 0:COLS] = (
                th[lev, row : row + 1] * w[1, lev, row : row + 1] * geo[0, row : row + 1, 0:COLS]
            )
        lat_copy(0, side, (1, BANDS - 1)[side]).start()

    def shrink(ch, values):
        for half in range(2):
            high, low = split(values * turn[half, :, 0:COLS])
            xhi[ch, half * ITEMS : (half + 1) * ITEMS, 0:COLS] = high
            xlo[ch, half * ITEMS : (half + 1) * ITEMS, 0:COLS] = low
        both = dot(shrink_ref[...], xhi[ch], ((1,), (1,)))
        rest = dot(shrink_ref[0:32], xlo[ch], ((1,), (1,)))
        u[ch] = both[0:RANK] + both[RANK : 2 * RANK] + rest[0:RANK]

    def u_copy(phase, t):
        q = (t + p) % PAIRS
        ch = phase * PAIRS + q
        to = worker(phase, q)
        remote = pltpu.make_async_remote_copy(
            src_ref=u.at[ch], dst_ref=zin.at[p], send_sem=u_sem, recv_sem=z_sem,
            device_id=(z, to), device_id_type=MESH,
        )
        return to, remote, pltpu.make_async_copy(u.at[ch], zin.at[p], z_sem)

    def send_u(phase):
        for t in range(PAIRS):
            to, remote, own = u_copy(phase, t)

            @pl.when(to != p)
            def _():
                remote.start()

            @pl.when(to == p)
            def _():
                own.start()

    @pl.when(polar)
    def _():
        for phase in range(2):

            def step(i, carry):
                shrink(phase * PAIRS + i, w[phase, pl.ds(2 * i, 2)].reshape(ITEMS, COLS))
                return carry

            lax.fori_loop(0, PAIRS, step, 0)
            send_u(phase)

    wait_edges(0)
    row_index = lax.broadcasted_iota(jnp.int32, (ROWS, WIDE), 0)
    for i in range(PAIRS):
        pair = slice(2 * i, 2 * i + 2)
        wide[:, 0:COLS] = (th[pair] * w[0, pair]).reshape(ITEMS, COLS)
        flux = jnp.concatenate([wide[:, 0:256], with_edges(0, i, wide[:, 256:WIDE])], axis=1)
        lon_diff = pltpu.roll(flux, WIDE - 1, 1) - pltpu.roll(flux, 1, 1)
        wide[:, 0:COLS] = (th[pair] * w[1, pair]).reshape(ITEMS, COLS)
        flux = wide[...] * geo[0]
        for k in range(2):
            lev = 2 * i + k
            cells = flux[k * ROWS : (k + 1) * ROWS]
            south = jnp.where(z == 0, 0.0, lat_in[0, 0, lev : lev + 1])
            north = jnp.where(z == BANDS - 1, 0.0, lat_in[0, 1, lev : lev + 1])
            up = jnp.where(row_index == ROWS - 1, north, pltpu.roll(cells, ROWS - 1, 0))
            down = jnp.where(row_index == 0, south, pltpu.roll(cells, 1, 0))
            change = geo[1, 0:ROWS] * (lon_diff[k * ROWS : (k + 1) * ROWS] + (up - down))
            th[lev] = th[lev] - change[:, 0:COLS]

    def local(ch, values):
        high = xhi[ch]
        low = xlo[ch]
        parts = dot(high, near[0], ((1,), (0,))) + dot(low, near[0], ((1,), (0,))) + dot(high, near[1], ((1,), (0,)))
        mixed = turn[1] * parts[0:ITEMS] - turn[0] * parts[ITEMS:]
        return mixed[:, 0:COLS] + turn[2, :, 0:COLS] * values

    def local_wind(phase):
        def step(i, carry):
            pair = pl.ds(2 * i, 2)
            result = local(phase * PAIRS + i, w[phase, pair].reshape(ITEMS, COLS))
            w[phase, pair] = result.reshape(2, ROWS, COLS)
            return carry

        lax.fori_loop(0, PAIRS, step, 0)

    def grown(ch):
        pltpu.make_async_copy(vr.at[ch], vr.at[ch], vr_sem.at[ch]).wait()
        values = vr[ch]
        high = values.astype(BF16).astype(F32)
        stack = jnp.concatenate([high, values - high, high, jnp.zeros((8, 2 * ITEMS), F32)], axis=0).astype(BF16)
        parts = dot(stack, grow_ref[...], ((0,), (0,)))
        mixed = turn[1] * parts[0:ITEMS] - turn[0] * parts[ITEMS:]
        return mixed[:, 0:COLS].reshape(2, ROWS, COLS)

    x = p // 8
    y = (p // 2) % 4
    core = p % 2
    parity = (x + y) % 2
    busy = polar & ((core == 0) | (parity == 0))
    mine = (2 * core + parity) * PAIRS + 2 * x + y // 2

    def v_copy(to):
        remote = pltpu.make_async_remote_copy(
            src_ref=vs.at[to], dst_ref=vr.at[mine], send_sem=v_sem, recv_sem=vr_sem.at[mine],
            device_id=(z, to), device_id_type=MESH,
        )
        return remote, pltpu.make_async_copy(vs.at[to], vr.at[mine], vr_sem.at[mine])

    @pl.when(polar)
    def _():
        def step(i, carry):
            shrink(2 * PAIRS + i, th[pl.ds(2 * i, 2)].reshape(ITEMS, COLS))
            return carry

        lax.fori_loop(0, PAIRS, step, 0)
        send_u(2)
        loads[3].wait()
        loads[4].wait()
        local_wind(0)

    @pl.when(busy)
    def _():
        pltpu.make_async_copy(zin, zin, z_sem).wait()
        high, low = split(zin[...].reshape(RING * RANK, 2 * ITEMS))
        zhi[...] = high
        zlo[...] = low
        part = RING * RANK // 4

        def step(m, carry):
            group = (x + m) % 4
            rows = pl.ds(pl.multiple_of(group * part, part), part)
            result = (
                dot(cross[0, rows], zhi[...], ((1,), (0,)))
                + dot(cross[0, rows], zlo[...], ((1,), (0,)))
                + dot(cross[1, rows], zhi[...], ((1,), (0,)))
            )
            vs[pl.ds(group * 8, 8)] = result.reshape(8, RANK, 2 * ITEMS)
            for j in range(8):
                to = group * 8 + (p + j) % 8
                remote, own = v_copy(to)

                @pl.when(to != p)
                def _():
                    remote.start()

                @pl.when(to == p)
                def _():
                    own.start()

            return carry

        lax.fori_loop(0, 4, step, 0)

    @pl.when(polar)
    def _():
        local_wind(1)

        def local_thick(i, carry):
            pair = pl.ds(2 * i, 2)
            th[pair] = local(2 * PAIRS + i, th[pair].reshape(ITEMS, COLS)).reshape(2, ROWS, COLS)
            return carry

        lax.fori_loop(0, PAIRS, local_thick, 0)

        def step(i, carry):
            pair = pl.ds(2 * i, 2)
            ext[pair, 0:ROWS, 0:COLS] = th[pair] + grown(2 * PAIRS + i)
            return carry

        lax.fori_loop(0, PAIRS, step, 0)

    @pl.when(jnp.logical_not(polar))
    def _():
        ext[:, 0:ROWS, 0:COLS] = th[...]

    def thick_first(i):
        return ext[2 * i : 2 * i + 2, 0:ROWS, 0:128].reshape(ITEMS, 128)[:, 0:1]

    def thick_last(i):
        return ext[2 * i : 2 * i + 2, 0:ROWS, 256:WIDE].reshape(ITEMS, 128)[:, COLS - 257 : COLS - 256]

    for side, row in ((0, ROWS - 1), (1, 0)):
        for lev in range(LEVELS):
            lat_out[1, side, lev : lev + 1, 0:COLS] = ext[lev, row : row + 1, 0:COLS]
        lat_copy(1, side, (1, BANDS - 1)[side]).start()
    send_lon(1, thick_first, thick_last)

    @pl.when(polar)
    def _():
        for phase in range(2):

            def step(i, carry):
                pair = pl.ds(2 * i, 2)
                w[phase, pair] = w[phase, pair] + grown(phase * PAIRS + i)
                return carry

            lax.fori_loop(0, PAIRS, step, 0)

    out_copy = pltpu.make_async_copy(w, out_hbm, done_sem.at[0])
    out_copy.start()

    wait_edges(1)
    for i in range(PAIRS):
        pair = slice(2 * i, 2 * i + 2)
        tile = ext[pair, 0:ROWS, 256:WIDE].reshape(ITEMS, 128)
        ext[pair, 0:ROWS, 256:WIDE] = with_edges(1, i, tile).reshape(2, ROWS, 128)
    for lev in range(LEVELS):
        ext[lev, ROWS : ROWS + 1] = jnp.where(z == BANDS - 1, 0.0, lat_in[1, 1, lev : lev + 1])
        ext[lev, ROWS + 7 : ROWS + 8] = jnp.where(z == 0, 0.0, lat_in[1, 0, lev : lev + 1])
    ext_copy = pltpu.make_async_copy(ext, ext_hbm, done_sem.at[1])
    ext_copy.start()

    @pl.when(polar)
    def _():
        for phase in range(3):
            for t in range(PAIRS):
                to, remote, own = u_copy(phase, t)

                @pl.when(to != p)
                def _():
                    remote.wait_send()

    @pl.when(busy)
    def _():
        def step(i, carry):
            remote, own = v_copy((p + i) % RING)
            remote.wait_send()
            return carry

        lax.fori_loop(1, RING, step, 0)

    @pl.when(jnp.logical_not(polar))
    def _():
        loads[3].wait()
        loads[4].wait()

    out_copy.wait()
    ext_copy.wait()


def gradient_kernel(ext_ref, wind_ref, thick_ref, out_ref):
    z, _ = place()
    _, metric = latitude_tables(z, (ROWS, WIDE))
    cells = ext_ref[0]
    lon_diff = (pltpu.roll(cells, WIDE - 1, 1) - pltpu.roll(cells, 1, 1))[0:ROWS]
    lat_diff = (pltpu.roll(cells, ROWS + 7, 0) - pltpu.roll(cells, 1, 0))[0:ROWS]
    thick_ref[0] = cells[0:ROWS, 0:COLS]
    out_ref[0, 0] = wind_ref[0, 0] - (press_coef * metric * lon_diff)[:, 0:COLS]
    out_ref[1, 0] = wind_ref[1, 0] - (press_coef * lat_diff)[:, 0:COLS]


def body(thickness, wind, cutoff, tables):
    shrink, grow, near, cross = tables
    any_space = pl.BlockSpec(memory_space=pl.ANY)
    vmem = pl.BlockSpec(memory_space=pltpu.VMEM)
    dma = pltpu.SemaphoreType.DMA
    ext, moved = pl.pallas_call(
        far_kernel,
        out_shape=(
            jax.ShapeDtypeStruct((LEVELS, ROWS + 8, WIDE), F32),
            jax.ShapeDtypeStruct((2, LEVELS, ROWS, COLS), F32),
        ),
        in_specs=[vmem, vmem, vmem, any_space, any_space, any_space, any_space],
        out_specs=(any_space, any_space),
        scratch_shapes=[
            pltpu.VMEM((LEVELS, ROWS, COLS), F32),
            pltpu.VMEM((2, LEVELS, ROWS, COLS), F32),
            pltpu.VMEM((LEVELS, ROWS + 8, WIDE), F32),
            pltpu.VMEM((CHUNKS, 2 * ITEMS, WIDE), BF16),
            pltpu.VMEM((CHUNKS, 2 * ITEMS, WIDE), BF16),
            pltpu.VMEM((3, ITEMS, WIDE), F32),
            pltpu.VMEM((2, ITEMS, WIDE), F32),
            pltpu.VMEM((ITEMS, WIDE), F32),
            pltpu.VMEM((2, WIDE, WIDE), BF16),
            pltpu.VMEM((2, RING * RANK, RING * RANK), BF16),
            pltpu.VMEM((CHUNKS, RANK, 2 * ITEMS), F32),
            pltpu.VMEM((RING, RANK, 2 * ITEMS), F32),
            pltpu.VMEM((RING, RANK, 2 * ITEMS), F32),
            pltpu.VMEM((CHUNKS, RANK, 2 * ITEMS), F32),
            pltpu.VMEM((RING * RANK, 2 * ITEMS), BF16),
            pltpu.VMEM((RING * RANK, 2 * ITEMS), BF16),
            pltpu.VMEM((2, ITEMS, 128), F32),
            pltpu.VMEM((2, 2, ITEMS, 128), F32),
            pltpu.VMEM((2, 2, LEVELS, WIDE), F32),
            pltpu.VMEM((2, 2, LEVELS, WIDE), F32),
            dma((5,)),
            dma,
            dma,
            dma,
            dma((CHUNKS,)),
            dma((2, 2)),
            dma((2, 2)),
            dma((2, 2)),
            dma((2, 2)),
            dma((2,)),
        ],
        compiler_params=pltpu.CompilerParams(
            collective_id=0, has_side_effects=True, vmem_limit_bytes=48 * 2**20
        ),
        name="far",
    )(cutoff.reshape(1, -1), shrink, grow, thickness, wind, near, cross)
    return pl.pallas_call(
        gradient_kernel,
        grid=(LEVELS,),
        out_shape=(
            jax.ShapeDtypeStruct((LEVELS, ROWS, COLS), F32),
            jax.ShapeDtypeStruct((2, LEVELS, ROWS, COLS), F32),
        ),
        in_specs=[
            pl.BlockSpec((1, ROWS + 8, WIDE), lambda i: (i, 0, 0)),
            pl.BlockSpec((2, 1, ROWS, COLS), lambda i: (0, i, 0, 0)),
        ],
        out_specs=(
            pl.BlockSpec((1, ROWS, COLS), lambda i: (i, 0, 0)),
            pl.BlockSpec((2, 1, ROWS, COLS), lambda i: (0, i, 0, 0)),
        ),
        name="gradient",
    )(ext, moved)


def solution(mesh):
    near, basis, cross = cauchy_tables()
    pad = WIDE - COLS
    near = jnp.stack(two_parts(np.pad(near.T, ((0, pad), (0, pad)))))
    cross = jnp.stack(two_parts(cross))
    high, low = two_parts(np.pad(basis.T, ((0, 0), (0, pad))))
    shrink = jnp.concatenate([high, low])
    grow = jnp.concatenate([high, high, low, jnp.zeros((8, WIDE), BF16)])
    in_specs = (P(None, "lat", "lon"), P(None, None, "lat", "lon"), P())
    out_specs = (P(None, "lat", "lon"), P(None, None, "lat", "lon"))

    def step(thickness, wind, cutoff):
        return body(thickness, wind, cutoff, (shrink, grow, near, cross))

    return jax.shard_map(step, mesh=mesh, in_specs=in_specs, out_specs=out_specs, check_vma=False)
```

```python
import functools
import math

import jax
import jax.numpy as jnp
import numpy as np
from jax import lax
from jax.experimental import pallas as pl
from jax.experimental.pallas import tpu as pltpu
from jax.sharding import PartitionSpec as P

MESH = pl.DeviceIdType.MESH
F32 = jnp.float32
BF16 = jnp.bfloat16

advect_coef = 0.05
press_coef = 0.1
FAR = 8
NEAR = 16
SUB = 128
SUB_RANKS = (13, 22, 13)
INNER = sum(SUB_RANKS)
SHORT = FAR + 2 * NEAR + INNER
SPREAD = INNER + 2 * NEAR
LEVELS = 16
ROWS = 64
COLS = 360
WIDE = 384
BANDS = 8
RING = 32
TOTAL = COLS * RING
PAIRS = LEVELS // 2
CHUNKS = 3 * PAIRS
STEP = 4
ITEMS = 2 * ROWS


def kernel_block(targets, sources):
    return 1.0 / (TOTAL * np.sin(np.pi * (targets[:, None] - sources[None]) / TOTAL))


def cauchy_tables():
    inside = np.arange(COLS)
    gap = np.arange(SUB)[:, None] - np.arange(SUB)[None]
    diagonal = np.where(gap == 0, 0.0, 1.0 / (TOTAL * np.sin(np.pi * gap / TOTAL) + (gap == 0)))
    far = np.linalg.svd(kernel_block(inside, np.arange(2 * COLS, TOTAL - COLS)), full_matrices=False)[0][:, :FAR]
    cross = np.zeros((RING, FAR, RING, FAR))
    for p in range(RING):
        for q in range(RING):
            if min((p - q) % RING, (q - p) % RING) >= 2:
                cross[p, :, q, :] = far.T @ kernel_block(p * COLS + inside, q * COLS + inside) @ far
    left, scale, right = np.linalg.svd(kernel_block(COLS + inside, inside))
    shorten = [far.T, right[:NEAR], left[:, :NEAR].T]
    from_left = (left * scale)[:, :NEAR].T
    from_right = -(scale[:, None] * right)[:NEAR]
    spread = []
    for k, rank in enumerate(SUB_RANKS):
        own = inside[k * SUB : (k + 1) * SUB]
        other = np.setdiff1d(inside, own)
        rows = np.linalg.svd(kernel_block(other, own), full_matrices=False)[2][:rank]
        padded = np.zeros((rank, COLS))
        padded[:, own] = rows
        shorten.append(padded)
        padded = np.zeros((rank, COLS))
        padded[:, other] = (kernel_block(other, own) @ rows.T).T
        spread.append(padded)
    spread += [from_left, from_right]
    return diagonal, np.concatenate(shorten), np.concatenate(spread), far.T, cross.reshape(RING * FAR, RING * FAR)


def widened(table):
    return np.pad(table, ((0, 0), (0, WIDE - COLS)))


def all_tables():
    diagonal, shorten, spread, far, cross = cauchy_tables()
    high, low = two_parts(diagonal.T)
    near = np.block([[high, low], [high, np.zeros_like(low)]])
    high, low = two_parts(widened(shorten))
    zero = np.zeros((SHORT, SUB), BF16)
    first = [high[:, k : k + SUB] for k in (0, SUB, 2 * SUB)]
    second = [low[:, k : k + SUB] for k in (0, SUB, 2 * SUB)]
    short = np.concatenate(
        [
            np.concatenate([part for f in first for part in (f, f)], axis=1),
            np.concatenate([part for f in second for part in (f, zero)], axis=1),
        ]
    )
    high, low = two_parts(widened(spread))
    early = np.concatenate([high, high, low])
    high, low = two_parts(widened(far))
    late = np.concatenate([high, high, low, np.zeros((FAR, WIDE), BF16)])
    return [jnp.asarray(t) for t in (near, short, early, late, np.stack(two_parts(cross)))]


def two_parts(table):
    table = table.astype(np.float32)
    high = table.astype(BF16)
    low = (table - high.astype(np.float32)).astype(BF16)
    return high, low


def split(values):
    high = values.astype(BF16)
    return high, (values - high.astype(F32)).astype(BF16)


def dot(left, right, dims):
    return lax.dot_general(left, right, (dims, ((), ())), preferred_element_type=F32)


def place():
    z = lax.axis_index("lat")
    p = lax.axis_index("lon")
    return z, p


def latitude_tables(z, shape):
    row = lax.broadcasted_iota(jnp.int32, shape, 0) + z * ROWS
    latitude = math.pi * ((row.astype(F32) + 0.5) / (ROWS * BANDS) - 0.5)
    cosine = jnp.cos(latitude)
    return cosine, 1.0 / jnp.maximum(cosine, 0.2)


def worker(phase, q):
    x = q // 2
    y = 2 * (q % 2) + (x + phase % 2) % 2
    return x * 8 + y * 2 + phase // 2


def far_kernel(
    cut_hbm, th_hbm, wind_hbm, near_hbm, short_hbm, early_hbm, late_hbm, cross_hbm,
    ext_hbm, out_hbm,
    cut_ref, th, w, ext, xs, turn, geo, wide, near, short, early, late, cross,
    inner, to_near, from_near, u, zin, vs, vr,
    lon_out, lon_in, lat_out, lat_in,
    load_sem, near_sem, nearr_sem, u_sem, z_sem, v_sem, vr_sem, lon_sem, lonr_sem, lat_sem, latr_sem, done_sem,
):
    z, p = place()
    polar = (z < 2) | (z >= 6)
    loads = [
        pltpu.make_async_copy(wind_hbm.at[0], w.at[0], load_sem.at[0]),
        pltpu.make_async_copy(th_hbm, th, load_sem.at[1]),
        pltpu.make_async_copy(wind_hbm.at[1], w.at[1], load_sem.at[2]),
        pltpu.make_async_copy(cut_hbm, cut_ref, load_sem.at[3]),
        pltpu.make_async_copy(short_hbm, short, load_sem.at[4]),
        pltpu.make_async_copy(near_hbm, near, load_sem.at[5]),
        pltpu.make_async_copy(early_hbm, early, load_sem.at[6]),
        pltpu.make_async_copy(cross_hbm, cross, load_sem.at[7]),
        pltpu.make_async_copy(late_hbm, late, load_sem.at[8]),
    ]
    for k in (3, 0, 1, 2, 4, 5, 6, 7, 8):
        loads[k].start()
    barrier = pltpu.get_barrier_semaphore()

    def greet(i, carry):
        pl.semaphore_signal(barrier, inc=1, device_id=(z, (p + i) % RING), device_id_type=MESH)
        return carry

    lax.fori_loop(1, RING, greet, 0)
    for dz in (1, BANDS - 1):
        pl.semaphore_signal(barrier, inc=1, device_id=((z + dz) % BANDS, p), device_id_type=MESH)

    cosine, metric = latitude_tables(z, (ROWS, WIDE))
    for half in range(2):
        geo[0, half * ROWS : (half + 1) * ROWS] = cosine
        geo[1, half * ROWS : (half + 1) * ROWS] = advect_coef * metric
    wide[...] = jnp.zeros((ITEMS, WIDE), F32)

    loads[3].wait()

    @pl.when(polar)
    def _():
        band = jnp.where(z < 2, z, z - 4)
        row = lax.broadcasted_iota(jnp.int32, (ROWS, 4 * ROWS), 0) + band * ROWS
        lane = lax.broadcasted_iota(jnp.int32, (ROWS, 4 * ROWS), 1)
        cuts = jnp.broadcast_to(cut_ref[...].astype(F32), (ROWS, 4 * ROWS))
        limit = jnp.sum(jnp.where(row == lane, cuts, 0.0), axis=1, keepdims=True)
        odd = 2.0 * limit + 1.0
        column = p * COLS + lax.broadcasted_iota(jnp.int32, (ROWS, WIDE), 1)
        product = jnp.broadcast_to(odd, (ROWS, WIDE)).astype(jnp.int32) * column
        laps = jnp.floor(product.astype(F32) * (0.5 / TOTAL)).astype(jnp.int32)
        angle = (product - laps * (2 * TOTAL)).astype(F32) * (math.pi / TOTAL)
        tables = (jnp.cos(angle), jnp.sin(angle), jnp.broadcast_to(odd * (1.0 / TOTAL), (ROWS, WIDE)))
        for k, table in enumerate(tables):
            for half in range(2):
                turn[k, half * ROWS : (half + 1) * ROWS] = table

        def clear(ch, carry):
            xs[ch, :, 4 * SUB :] = jnp.zeros((2 * ITEMS, 2 * SUB), BF16)
            return carry

        lax.fori_loop(0, CHUNKS, clear, 0)

    pl.semaphore_wait(barrier, RING + 1)

    lane = lax.broadcasted_iota(jnp.int32, (ITEMS, 128), 1)

    def send_lon(kind, first, last):
        edges = jnp.zeros((ITEMS, 128), F32)
        for i in range(PAIRS):
            edges = jnp.where(lane == i, first(i), edges)
            edges = jnp.where(lane == PAIRS + i, last(i), edges)
        lon_out[kind] = edges
        for side, step in ((0, 1), (1, RING - 1)):
            lon_copy(kind, side, step).start()

    def lon_copy(kind, side, step):
        return pltpu.make_async_remote_copy(
            src_ref=lon_out.at[kind], dst_ref=lon_in.at[kind, side],
            send_sem=lon_sem.at[kind, side], recv_sem=lonr_sem.at[kind, side],
            device_id=(z, (p + step) % RING), device_id_type=MESH,
        )

    def lat_copy(kind, side, step):
        return pltpu.make_async_remote_copy(
            src_ref=lat_out.at[kind, side], dst_ref=lat_in.at[kind, side],
            send_sem=lat_sem.at[kind, side], recv_sem=latr_sem.at[kind, side],
            device_id=((z + step) % BANDS, p), device_id_type=MESH,
        )

    def wait_edges(kind):
        for side, step in ((0, 1), (1, RING - 1)):
            lon_copy(kind, side, step).wait()
        for side, step in ((0, 1), (1, BANDS - 1)):
            lat_copy(kind, side, step).wait()

    def with_edges(kind, i, tile):
        left = lon_in[kind, 0, :, PAIRS + i : PAIRS + i + 1]
        right = lon_in[kind, 1, :, i : i + 1]
        return jnp.where(lane == COLS - 256, right, jnp.where(lane == 127, left, tile))

    loads[0].wait()
    loads[1].wait()

    def flux_first(i):
        return (th[2 * i : 2 * i + 2, :, 0:128] * w[0, 2 * i : 2 * i + 2, :, 0:128]).reshape(ITEMS, 128)[:, 0:1]

    def flux_last(i):
        tile = th[2 * i : 2 * i + 2, :, 256:COLS] * w[0, 2 * i : 2 * i + 2, :, 256:COLS]
        return tile.reshape(ITEMS, COLS - 256)[:, COLS - 257 : COLS - 256]

    send_lon(0, flux_first, flux_last)
    loads[2].wait()
    for side, row in ((0, ROWS - 1), (1, 0)):
        for lev in range(LEVELS):
            lat_out[0, side, lev : lev + 1, 0:COLS] = (
                th[lev, row : row + 1] * w[1, lev, row : row + 1] * geo[0, row : row + 1, 0:COLS]
            )
        lat_copy(0, side, (1, BANDS - 1)[side]).start()

    def shrink(ch, values):
        for half in range(2):
            rows = slice(half * ITEMS, (half + 1) * ITEMS)
            high, low = split(values * turn[half, :, 0:COLS])
            for k in range(3):
                size = min(SUB, COLS - k * SUB)
                xs[ch, rows, 2 * k * SUB : 2 * k * SUB + size] = high[:, k * SUB : k * SUB + size]
                xs[ch, rows, (2 * k + 1) * SUB : (2 * k + 1) * SUB + size] = low[:, k * SUB : k * SUB + size]
        both = dot(short[...], xs[ch], ((1,), (1,)))
        both = both[0:SHORT] + both[SHORT:]
        u[ch] = both[0:FAR]
        to_near[0, ch] = both[FAR : FAR + NEAR]
        to_near[1, ch] = both[FAR + NEAR : FAR + 2 * NEAR]
        inner[ch] = both[FAR + 2 * NEAR :]

    def near_copy(phase, side):
        part = pl.ds(phase * PAIRS, PAIRS)
        return pltpu.make_async_remote_copy(
            src_ref=to_near.at[side, part], dst_ref=from_near.at[side, part],
            send_sem=near_sem.at[phase, side], recv_sem=nearr_sem.at[phase, side],
            device_id=(z, (p + (1, RING - 1)[side]) % RING), device_id_type=MESH,
        )

    def u_copy(phase, t):
        q = (t + p) % PAIRS
        ch = phase * PAIRS + q
        to = worker(phase, q)
        remote = pltpu.make_async_remote_copy(
            src_ref=u.at[ch], dst_ref=zin.at[p], send_sem=u_sem, recv_sem=z_sem,
            device_id=(z, to), device_id_type=MESH,
        )
        return to, remote, pltpu.make_async_copy(u.at[ch], zin.at[p], z_sem)

    def send_u(phase):
        for t in range(PAIRS):
            to, remote, own = u_copy(phase, t)

            @pl.when(to != p)
            def _():
                remote.start()

            @pl.when(to == p)
            def _():
                own.start()

    @pl.when(polar)
    def _():
        loads[4].wait()
        for phase in range(2):

            def step(i, carry):
                shrink(phase * PAIRS + i, w[phase, pl.ds(2 * i, 2)].reshape(ITEMS, COLS))
                return carry

            lax.fori_loop(0, PAIRS, step, 0)
            send_u(phase)
            for side in range(2):
                near_copy(phase, side).start()

    wait_edges(0)
    row_index = lax.broadcasted_iota(jnp.int32, (ROWS, WIDE), 0)
    for i in range(PAIRS):
        pair = slice(2 * i, 2 * i + 2)
        wide[:, 0:COLS] = (th[pair] * w[0, pair]).reshape(ITEMS, COLS)
        flux = jnp.concatenate([wide[:, 0:256], with_edges(0, i, wide[:, 256:WIDE])], axis=1)
        lon_diff = pltpu.roll(flux, WIDE - 1, 1) - pltpu.roll(flux, 1, 1)
        wide[:, 0:COLS] = (th[pair] * w[1, pair]).reshape(ITEMS, COLS)
        flux = wide[...] * geo[0]
        for k in range(2):
            lev = 2 * i + k
            cells = flux[k * ROWS : (k + 1) * ROWS]
            south = jnp.where(z == 0, 0.0, lat_in[0, 0, lev : lev + 1])
            north = jnp.where(z == BANDS - 1, 0.0, lat_in[0, 1, lev : lev + 1])
            up = jnp.where(row_index == ROWS - 1, north, pltpu.roll(cells, ROWS - 1, 0))
            down = jnp.where(row_index == 0, south, pltpu.roll(cells, 1, 0))
            change = geo[1, 0:ROWS] * (lon_diff[k * ROWS : (k + 1) * ROWS] + (up - down))
            th[lev] = th[lev] - change[:, 0:COLS]

    first_sign = jnp.where(p == 0, -1.0, 1.0).astype(F32)
    last_sign = jnp.where(p == RING - 1, -1.0, 1.0).astype(F32)

    def turned_back(parts):
        mixed = turn[1] * parts[0:ITEMS] - turn[0] * parts[ITEMS:]
        return mixed[:, 0:COLS]

    def local(ch, values):
        pieces = []
        for k in range(3):
            both = dot(xs[ch, :, 2 * k * SUB : (2 * k + 2) * SUB], near[...], ((1,), (0,)))
            pieces.append(both[:, 0:SUB] + both[:, SUB:])
        stack = jnp.concatenate([inner[ch], first_sign * from_near[0, ch], last_sign * from_near[1, ch]], axis=0)
        high = stack.astype(BF16).astype(F32)
        stack = jnp.concatenate([high, stack - high, high], axis=0).astype(BF16)
        parts = jnp.concatenate(pieces, axis=1) + dot(stack, early[...], ((0,), (0,)))
        return turned_back(parts) + turn[2, :, 0:COLS] * values

    def local_wind(phase):
        for side in range(2):
            near_copy(phase, side).wait()

        def step(i, carry):
            pair = pl.ds(2 * i, 2)
            result = local(phase * PAIRS + i, w[phase, pair].reshape(ITEMS, COLS))
            w[phase, pair] = result.reshape(2, ROWS, COLS)
            return carry

        lax.fori_loop(0, PAIRS, step, 0)

    def grown(ch):
        pltpu.make_async_copy(vr.at[ch], vr.at[ch], vr_sem.at[ch]).wait()
        values = vr[ch]
        high = values.astype(BF16).astype(F32)
        stack = jnp.concatenate([high, values - high, high, jnp.zeros((FAR, 2 * ITEMS), F32)], axis=0).astype(BF16)
        return turned_back(dot(stack, late[...], ((0,), (0,)))).reshape(2, ROWS, COLS)

    x = p // 8
    y = (p // 2) % 4
    core = p % 2
    parity = (x + y) % 2
    busy = polar & ((core == 0) | (parity == 0))
    mine = (2 * core + parity) * PAIRS + 2 * x + y // 2

    def v_copy(to):
        remote = pltpu.make_async_remote_copy(
            src_ref=vs.at[to], dst_ref=vr.at[mine], send_sem=v_sem, recv_sem=vr_sem.at[mine],
            device_id=(z, to), device_id_type=MESH,
        )
        return remote, pltpu.make_async_copy(vs.at[to], vr.at[mine], vr_sem.at[mine])

    @pl.when(polar)
    def _():
        def step(i, carry):
            shrink(2 * PAIRS + i, th[pl.ds(2 * i, 2)].reshape(ITEMS, COLS))
            return carry

        lax.fori_loop(0, PAIRS, step, 0)
        send_u(2)
        for side in range(2):
            near_copy(2, side).start()
        for k in range(5, 9):
            loads[k].wait()
        local_wind(0)

    @pl.when(busy)
    def _():
        pltpu.make_async_copy(zin, zin, z_sem).wait()
        high, low = split(zin[...].reshape(RING * FAR, 2 * ITEMS))
        result = (
            dot(cross[0], high, ((1,), (0,)))
            + dot(cross[0], low, ((1,), (0,)))
            + dot(cross[1], high, ((1,), (0,)))
        )
        vs[...] = result.reshape(RING, FAR, 2 * ITEMS)
        remote, own = v_copy(p)
        own.start()

        def step(i, carry):
            remote, own = v_copy((p + i) % RING)
            remote.start()
            return carry

        lax.fori_loop(1, RING, step, 0)

    @pl.when(polar)
    def _():
        local_wind(1)
        for side in range(2):
            near_copy(2, side).wait()

        def local_thick(i, carry):
            pair = pl.ds(2 * i, 2)
            th[pair] = local(2 * PAIRS + i, th[pair].reshape(ITEMS, COLS)).reshape(2, ROWS, COLS)
            return carry

        lax.fori_loop(0, PAIRS, local_thick, 0)

        def step(i, carry):
            pair = pl.ds(2 * i, 2)
            ext[pair, 0:ROWS, 0:COLS] = th[pair] + grown(2 * PAIRS + i)
            return carry

        lax.fori_loop(0, PAIRS, step, 0)

    @pl.when(jnp.logical_not(polar))
    def _():
        ext[:, 0:ROWS, 0:COLS] = th[...]

    def thick_first(i):
        return ext[2 * i : 2 * i + 2, 0:ROWS, 0:128].reshape(ITEMS, 128)[:, 0:1]

    def thick_last(i):
        return ext[2 * i : 2 * i + 2, 0:ROWS, 256:WIDE].reshape(ITEMS, 128)[:, COLS - 257 : COLS - 256]

    for side, row in ((0, ROWS - 1), (1, 0)):
        for lev in range(LEVELS):
            lat_out[1, side, lev : lev + 1, 0:COLS] = ext[lev, row : row + 1, 0:COLS]
        lat_copy(1, side, (1, BANDS - 1)[side]).start()
    send_lon(1, thick_first, thick_last)

    @pl.when(polar)
    def _():
        for phase in range(2):

            def step(i, carry):
                pair = pl.ds(2 * i, 2)
                w[phase, pair] = w[phase, pair] + grown(phase * PAIRS + i)
                return carry

            lax.fori_loop(0, PAIRS, step, 0)

    out_copy = pltpu.make_async_copy(w, out_hbm, done_sem.at[0])
    out_copy.start()

    wait_edges(1)
    for i in range(PAIRS):
        pair = slice(2 * i, 2 * i + 2)
        tile = ext[pair, 0:ROWS, 256:WIDE].reshape(ITEMS, 128)
        ext[pair, 0:ROWS, 256:WIDE] = with_edges(1, i, tile).reshape(2, ROWS, 128)
    for lev in range(LEVELS):
        ext[lev, ROWS : ROWS + 1] = jnp.where(z == BANDS - 1, 0.0, lat_in[1, 1, lev : lev + 1])
        ext[lev, ROWS + 7 : ROWS + 8] = jnp.where(z == 0, 0.0, lat_in[1, 0, lev : lev + 1])
    ext_copy = pltpu.make_async_copy(ext, ext_hbm, done_sem.at[1])
    ext_copy.start()

    @pl.when(polar)
    def _():
        for phase in range(3):
            for t in range(PAIRS):
                to, remote, own = u_copy(phase, t)

                @pl.when(to != p)
                def _():
                    remote.wait_send()

    @pl.when(busy)
    def _():
        def step(i, carry):
            remote, own = v_copy((p + i) % RING)
            remote.wait_send()
            return carry

        lax.fori_loop(1, RING, step, 0)

    @pl.when(jnp.logical_not(polar))
    def _():
        for k in range(4, 9):
            loads[k].wait()

    out_copy.wait()
    ext_copy.wait()


def gradient_kernel(ext_ref, wind_ref, thick_ref, out_ref, geo):
    z, _ = place()

    @pl.when(pl.program_id(0) == 0)
    def _():
        geo[...] = press_coef * latitude_tables(z, (ROWS, WIDE))[1]

    for k in range(STEP):
        cells = ext_ref[k]
        lon_diff = pltpu.roll(cells, WIDE - 1, 1) - pltpu.roll(cells, 1, 1)
        lat_diff = pltpu.roll(cells, ROWS + 7, 0) - pltpu.roll(cells, 1, 0)
        thick_ref[k] = cells[0:ROWS, 0:COLS]
        out_ref[0, k] = wind_ref[0, k] - (geo[...] * lon_diff[0:ROWS])[:, 0:COLS]
        out_ref[1, k] = wind_ref[1, k] - (press_coef * lat_diff[0:ROWS])[:, 0:COLS]


def body(thickness, wind, cutoff, tables):
    near, short, early, late, cross = tables
    any_space = pl.BlockSpec(memory_space=pl.ANY)
    dma = pltpu.SemaphoreType.DMA
    ext, moved = pl.pallas_call(
        far_kernel,
        out_shape=(
            jax.ShapeDtypeStruct((LEVELS, ROWS + 8, WIDE), F32),
            jax.ShapeDtypeStruct((2, LEVELS, ROWS, COLS), F32),
        ),
        in_specs=[any_space] * 8,
        out_specs=(any_space, any_space),
        scratch_shapes=[
            pltpu.VMEM((1, 4 * ROWS), jnp.int32),
            pltpu.VMEM((LEVELS, ROWS, COLS), F32),
            pltpu.VMEM((2, LEVELS, ROWS, COLS), F32),
            pltpu.VMEM((LEVELS, ROWS + 8, WIDE), F32),
            pltpu.VMEM((CHUNKS, 2 * ITEMS, 2 * WIDE), BF16),
            pltpu.VMEM((3, ITEMS, WIDE), F32),
            pltpu.VMEM((2, ITEMS, WIDE), F32),
            pltpu.VMEM((ITEMS, WIDE), F32),
            pltpu.VMEM(near.shape, BF16),
            pltpu.VMEM(short.shape, BF16),
            pltpu.VMEM(early.shape, BF16),
            pltpu.VMEM(late.shape, BF16),
            pltpu.VMEM(cross.shape, BF16),
            pltpu.VMEM((CHUNKS, INNER, 2 * ITEMS), F32),
            pltpu.VMEM((2, CHUNKS, NEAR, 2 * ITEMS), F32),
            pltpu.VMEM((2, CHUNKS, NEAR, 2 * ITEMS), F32),
            pltpu.VMEM((CHUNKS, FAR, 2 * ITEMS), F32),
            pltpu.VMEM((RING, FAR, 2 * ITEMS), F32),
            pltpu.VMEM((RING, FAR, 2 * ITEMS), F32),
            pltpu.VMEM((CHUNKS, FAR, 2 * ITEMS), F32),
            pltpu.VMEM((2, ITEMS, 128), F32),
            pltpu.VMEM((2, 2, ITEMS, 128), F32),
            pltpu.VMEM((2, 2, LEVELS, WIDE), F32),
            pltpu.VMEM((2, 2, LEVELS, WIDE), F32),
            dma((9,)),
            dma((3, 2)),
            dma((3, 2)),
            dma,
            dma,
            dma,
            dma((CHUNKS,)),
            dma((2, 2)),
            dma((2, 2)),
            dma((2, 2)),
            dma((2, 2)),
            dma((2,)),
        ],
        compiler_params=pltpu.CompilerParams(
            collective_id=0, has_side_effects=True, vmem_limit_bytes=60 * 2**20
        ),
        name="far",
    )(cutoff.reshape(1, -1), thickness, wind, near, short, early, late, cross)
    return pl.pallas_call(
        gradient_kernel,
        grid=(LEVELS // STEP,),
        out_shape=(
            jax.ShapeDtypeStruct((LEVELS, ROWS, COLS), F32),
            jax.ShapeDtypeStruct((2, LEVELS, ROWS, COLS), F32),
        ),
        in_specs=[
            pl.BlockSpec((STEP, ROWS + 8, WIDE), lambda i: (i, 0, 0)),
            pl.BlockSpec((2, STEP, ROWS, COLS), lambda i: (0, i, 0, 0)),
        ],
        out_specs=(
            pl.BlockSpec((STEP, ROWS, COLS), lambda i: (i, 0, 0)),
            pl.BlockSpec((2, STEP, ROWS, COLS), lambda i: (0, i, 0, 0)),
        ),
        scratch_shapes=[pltpu.VMEM((ROWS, WIDE), F32)],
        name="gradient",
    )(ext, moved)


def solution(mesh):
    tables = all_tables()
    in_specs = (P(None, "lat", "lon"), P(None, None, "lat", "lon"), P())
    out_specs = (P(None, "lat", "lon"), P(None, None, "lat", "lon"))

    def step(thickness, wind, cutoff):
        return body(thickness, wind, cutoff, tables)

    return jax.shard_map(step, mesh=mesh, in_specs=in_specs, out_specs=out_specs, check_vma=False)
```

```python
import functools
import math

import jax
import jax.numpy as jnp
import numpy as np
from jax import lax
from jax.experimental import pallas as pl
from jax.experimental.pallas import tpu as pltpu
from jax.sharding import PartitionSpec as P

MESH = pl.DeviceIdType.MESH
F32 = jnp.float32
BF16 = jnp.bfloat16

advect_coef = 0.05
press_coef = 0.1
FAR = 8
NEAR = 16
SUB = 128
SUB_RANKS = (13, 22, 13)
INNER = sum(SUB_RANKS)
SHORT = FAR + 2 * NEAR + INNER
SPREAD = INNER + 2 * NEAR
LEVELS = 16
ROWS = 64
COLS = 360
WIDE = 384
BANDS = 8
RING = 32
TOTAL = COLS * RING
PAIRS = LEVELS // 2
CHUNKS = 3 * PAIRS
STEP = 4
ITEMS = 2 * ROWS


def kernel_block(targets, sources):
    return 1.0 / (TOTAL * np.sin(np.pi * (targets[:, None] - sources[None]) / TOTAL))


def cauchy_tables():
    inside = np.arange(COLS)
    gap = np.arange(SUB)[:, None] - np.arange(SUB)[None]
    diagonal = np.where(gap == 0, 0.0, 1.0 / (TOTAL * np.sin(np.pi * gap / TOTAL) + (gap == 0)))
    far = np.linalg.svd(kernel_block(inside, np.arange(2 * COLS, TOTAL - COLS)), full_matrices=False)[0][:, :FAR]
    cross = np.zeros((RING, FAR, RING, FAR))
    for p in range(RING):
        for q in range(RING):
            if min((p - q) % RING, (q - p) % RING) >= 2:
                cross[p, :, q, :] = far.T @ kernel_block(p * COLS + inside, q * COLS + inside) @ far
    left, scale, right = np.linalg.svd(kernel_block(COLS + inside, inside))
    shorten = [far.T, right[:NEAR], left[:, :NEAR].T]
    from_left = (left * scale)[:, :NEAR].T
    from_right = -(scale[:, None] * right)[:NEAR]
    spread = []
    for k, rank in enumerate(SUB_RANKS):
        own = inside[k * SUB : (k + 1) * SUB]
        other = np.setdiff1d(inside, own)
        rows = np.linalg.svd(kernel_block(other, own), full_matrices=False)[2][:rank]
        padded = np.zeros((rank, COLS))
        padded[:, own] = rows
        shorten.append(padded)
        padded = np.zeros((rank, COLS))
        padded[:, other] = (kernel_block(other, own) @ rows.T).T
        spread.append(padded)
    spread += [from_left, from_right]
    return diagonal, np.concatenate(shorten), np.concatenate(spread), far.T, cross.reshape(RING * FAR, RING * FAR)


def widened(table):
    return np.pad(table, ((0, 0), (0, WIDE - COLS)))


def all_tables():
    diagonal, shorten, spread, far, cross = cauchy_tables()
    high, low = two_parts(diagonal.T)
    near = np.block([[high, low], [high, np.zeros_like(low)]])
    high, low = two_parts(widened(shorten))
    zero = np.zeros((SHORT, SUB), BF16)
    first = [high[:, k : k + SUB] for k in (0, SUB, 2 * SUB)]
    second = [low[:, k : k + SUB] for k in (0, SUB, 2 * SUB)]
    short = np.concatenate(
        [
            np.concatenate([part for f in first for part in (f, f)], axis=1),
            np.concatenate([part for f in second for part in (f, zero)], axis=1),
        ]
    )
    high, low = two_parts(widened(spread))
    early = np.concatenate([high, high, low])
    high, low = two_parts(widened(far))
    late = np.concatenate([high, high, low, np.zeros((FAR, WIDE), BF16)])
    return [jnp.asarray(t) for t in (near, short, early, late, np.stack(two_parts(cross)))]


def two_parts(table):
    table = table.astype(np.float32)
    high = table.astype(BF16)
    low = (table - high.astype(np.float32)).astype(BF16)
    return high, low


def split(values):
    high = values.astype(BF16)
    return high, (values - high.astype(F32)).astype(BF16)


def dot(left, right, dims):
    return lax.dot_general(left, right, (dims, ((), ())), preferred_element_type=F32)


def place():
    z = lax.axis_index("lat")
    p = lax.axis_index("lon")
    return z, p


def latitude_tables(z, shape):
    row = lax.broadcasted_iota(jnp.int32, shape, 0) + z * ROWS
    latitude = math.pi * ((row.astype(F32) + 0.5) / (ROWS * BANDS) - 0.5)
    cosine = jnp.cos(latitude)
    return cosine, 1.0 / jnp.maximum(cosine, 0.2)


def worker(phase, q):
    x = q // 2
    y = 2 * (q % 2) + (x + phase % 2) % 2
    return x * 8 + y * 2 + phase // 2


def far_kernel(
    cut_hbm, th_hbm, wind_hbm, near_hbm, short_hbm, early_hbm, late_hbm, cross_hbm,
    ext, w,
    cut_ref, th, xs, turn, geo, wide, near, short, early, late, cross,
    inner, to_near, from_near, u, zin, vs, vr,
    lon_out, lon_in, lat_out, lat_in,
    load_sem, near_sem, nearr_sem, u_sem, z_sem, v_sem, vr_sem, lon_sem, lonr_sem, lat_sem, latr_sem,
):
    z, p = place()
    polar = (z < 2) | (z >= 6)
    loads = [
        pltpu.make_async_copy(wind_hbm.at[0], w.at[0], load_sem.at[0]),
        pltpu.make_async_copy(th_hbm, th, load_sem.at[1]),
        pltpu.make_async_copy(wind_hbm.at[1], w.at[1], load_sem.at[2]),
        pltpu.make_async_copy(cut_hbm, cut_ref, load_sem.at[3]),
        pltpu.make_async_copy(short_hbm, short, load_sem.at[4]),
        pltpu.make_async_copy(near_hbm, near, load_sem.at[5]),
        pltpu.make_async_copy(early_hbm, early, load_sem.at[6]),
        pltpu.make_async_copy(cross_hbm, cross, load_sem.at[7]),
        pltpu.make_async_copy(late_hbm, late, load_sem.at[8]),
    ]
    for k in (3, 0, 1, 2, 4, 5, 6, 7, 8):
        loads[k].start()
    barrier = pltpu.get_barrier_semaphore()

    def greet(i, carry):
        pl.semaphore_signal(barrier, inc=1, device_id=(z, (p + i) % RING), device_id_type=MESH)
        return carry

    lax.fori_loop(1, RING, greet, 0)
    for dz in (1, BANDS - 1):
        pl.semaphore_signal(barrier, inc=1, device_id=((z + dz) % BANDS, p), device_id_type=MESH)

    cosine, metric = latitude_tables(z, (ROWS, WIDE))
    for half in range(2):
        geo[0, half * ROWS : (half + 1) * ROWS] = cosine
        geo[1, half * ROWS : (half + 1) * ROWS] = advect_coef * metric
    wide[...] = jnp.zeros((ITEMS, WIDE), F32)

    loads[3].wait()

    @pl.when(polar)
    def _():
        band = jnp.where(z < 2, z, z - 4)
        row = lax.broadcasted_iota(jnp.int32, (ROWS, 4 * ROWS), 0) + band * ROWS
        lane = lax.broadcasted_iota(jnp.int32, (ROWS, 4 * ROWS), 1)
        cuts = jnp.broadcast_to(cut_ref[...].astype(F32), (ROWS, 4 * ROWS))
        limit = jnp.sum(jnp.where(row == lane, cuts, 0.0), axis=1, keepdims=True)
        odd = 2.0 * limit + 1.0
        column = p * COLS + lax.broadcasted_iota(jnp.int32, (ROWS, WIDE), 1)
        product = jnp.broadcast_to(odd, (ROWS, WIDE)).astype(jnp.int32) * column
        laps = jnp.floor(product.astype(F32) * (0.5 / TOTAL)).astype(jnp.int32)
        angle = (product - laps * (2 * TOTAL)).astype(F32) * (math.pi / TOTAL)
        tables = (jnp.cos(angle), jnp.sin(angle), jnp.broadcast_to(odd * (1.0 / TOTAL), (ROWS, WIDE)))
        for k, table in enumerate(tables):
            for half in range(2):
                turn[k, half * ROWS : (half + 1) * ROWS] = table

        def clear(ch, carry):
            xs[ch, :, 4 * SUB :] = jnp.zeros((2 * ITEMS, 2 * SUB), BF16)
            return carry

        lax.fori_loop(0, CHUNKS, clear, 0)

    pl.semaphore_wait(barrier, RING + 1)

    lane = lax.broadcasted_iota(jnp.int32, (ITEMS, 128), 1)

    def send_lon(kind, first, last):
        edges = jnp.zeros((ITEMS, 128), F32)
        for i in range(PAIRS):
            edges = jnp.where(lane == i, first(i), edges)
            edges = jnp.where(lane == PAIRS + i, last(i), edges)
        lon_out[kind] = edges
        for side, step in ((0, 1), (1, RING - 1)):
            lon_copy(kind, side, step).start()

    def lon_copy(kind, side, step):
        return pltpu.make_async_remote_copy(
            src_ref=lon_out.at[kind], dst_ref=lon_in.at[kind, side],
            send_sem=lon_sem.at[kind, side], recv_sem=lonr_sem.at[kind, side],
            device_id=(z, (p + step) % RING), device_id_type=MESH,
        )

    def lat_copy(kind, side, step):
        return pltpu.make_async_remote_copy(
            src_ref=lat_out.at[kind, side], dst_ref=lat_in.at[kind, side],
            send_sem=lat_sem.at[kind, side], recv_sem=latr_sem.at[kind, side],
            device_id=((z + step) % BANDS, p), device_id_type=MESH,
        )

    def wait_edges(kind):
        for side, step in ((0, 1), (1, RING - 1)):
            lon_copy(kind, side, step).wait()
        for side, step in ((0, 1), (1, BANDS - 1)):
            lat_copy(kind, side, step).wait()

    def with_edges(kind, i, tile):
        left = lon_in[kind, 0, :, PAIRS + i : PAIRS + i + 1]
        right = lon_in[kind, 1, :, i : i + 1]
        return jnp.where(lane == COLS - 256, right, jnp.where(lane == 127, left, tile))

    loads[0].wait()
    loads[1].wait()

    def flux_first(i):
        return (th[2 * i : 2 * i + 2, :, 0:128] * w[0, 2 * i : 2 * i + 2, :, 0:128]).reshape(ITEMS, 128)[:, 0:1]

    def flux_last(i):
        tile = th[2 * i : 2 * i + 2, :, 256:COLS] * w[0, 2 * i : 2 * i + 2, :, 256:COLS]
        return tile.reshape(ITEMS, COLS - 256)[:, COLS - 257 : COLS - 256]

    send_lon(0, flux_first, flux_last)
    loads[2].wait()
    for side, row in ((0, ROWS - 1), (1, 0)):
        for lev in range(LEVELS):
            lat_out[0, side, lev : lev + 1, 0:COLS] = (
                th[lev, row : row + 1] * w[1, lev, row : row + 1] * geo[0, row : row + 1, 0:COLS]
            )
        lat_copy(0, side, (1, BANDS - 1)[side]).start()

    def shrink(ch, values):
        for half in range(2):
            rows = slice(half * ITEMS, (half + 1) * ITEMS)
            high, low = split(values * turn[half, :, 0:COLS])
            for k in range(3):
                size = min(SUB, COLS - k * SUB)
                xs[ch, rows, 2 * k * SUB : 2 * k * SUB + size] = high[:, k * SUB : k * SUB + size]
                xs[ch, rows, (2 * k + 1) * SUB : (2 * k + 1) * SUB + size] = low[:, k * SUB : k * SUB + size]
        both = dot(short[...], xs[ch], ((1,), (1,)))
        both = both[0:SHORT] + both[SHORT:]
        u[ch] = both[0:FAR]
        to_near[0, ch] = both[FAR : FAR + NEAR]
        to_near[1, ch] = both[FAR + NEAR : FAR + 2 * NEAR]
        inner[ch] = both[FAR + 2 * NEAR :]

    def near_copy(phase, side):
        part = pl.ds(phase * PAIRS, PAIRS)
        return pltpu.make_async_remote_copy(
            src_ref=to_near.at[side, part], dst_ref=from_near.at[side, part],
            send_sem=near_sem.at[phase, side], recv_sem=nearr_sem.at[phase, side],
            device_id=(z, (p + (1, RING - 1)[side]) % RING), device_id_type=MESH,
        )

    def u_copy(phase, t):
        q = (t + p) % PAIRS
        ch = phase * PAIRS + q
        to = worker(phase, q)
        remote = pltpu.make_async_remote_copy(
            src_ref=u.at[ch], dst_ref=zin.at[p], send_sem=u_sem, recv_sem=z_sem,
            device_id=(z, to), device_id_type=MESH,
        )
        return to, remote, pltpu.make_async_copy(u.at[ch], zin.at[p], z_sem)

    def send_u(phase):
        for t in range(PAIRS):
            to, remote, own = u_copy(phase, t)

            @pl.when(to != p)
            def _():
                remote.start()

            @pl.when(to == p)
            def _():
                own.start()

    @pl.when(polar)
    def _():
        loads[4].wait()
        for phase in range(2):

            def step(i, carry):
                shrink(phase * PAIRS + i, w[phase, pl.ds(2 * i, 2)].reshape(ITEMS, COLS))
                return carry

            lax.fori_loop(0, PAIRS, step, 0)
            send_u(phase)
            for side in range(2):
                near_copy(phase, side).start()

    wait_edges(0)
    row_index = lax.broadcasted_iota(jnp.int32, (ROWS, WIDE), 0)
    for i in range(PAIRS):
        pair = slice(2 * i, 2 * i + 2)
        wide[:, 0:COLS] = (th[pair] * w[0, pair]).reshape(ITEMS, COLS)
        flux = jnp.concatenate([wide[:, 0:256], with_edges(0, i, wide[:, 256:WIDE])], axis=1)
        lon_diff = pltpu.roll(flux, WIDE - 1, 1) - pltpu.roll(flux, 1, 1)
        wide[:, 0:COLS] = (th[pair] * w[1, pair]).reshape(ITEMS, COLS)
        flux = wide[...] * geo[0]
        for k in range(2):
            lev = 2 * i + k
            cells = flux[k * ROWS : (k + 1) * ROWS]
            south = jnp.where(z == 0, 0.0, lat_in[0, 0, lev : lev + 1])
            north = jnp.where(z == BANDS - 1, 0.0, lat_in[0, 1, lev : lev + 1])
            up = jnp.where(row_index == ROWS - 1, north, pltpu.roll(cells, ROWS - 1, 0))
            down = jnp.where(row_index == 0, south, pltpu.roll(cells, 1, 0))
            change = geo[1, 0:ROWS] * (lon_diff[k * ROWS : (k + 1) * ROWS] + (up - down))
            th[lev] = th[lev] - change[:, 0:COLS]

    first_sign = jnp.where(p == 0, -1.0, 1.0).astype(F32)
    last_sign = jnp.where(p == RING - 1, -1.0, 1.0).astype(F32)

    def turned_back(parts):
        mixed = turn[1] * parts[0:ITEMS] - turn[0] * parts[ITEMS:]
        return mixed[:, 0:COLS]

    def local(ch, values):
        pieces = []
        for k in range(3):
            both = dot(xs[ch, :, 2 * k * SUB : (2 * k + 2) * SUB], near[...], ((1,), (0,)))
            pieces.append(both[:, 0:SUB] + both[:, SUB:])
        stack = jnp.concatenate([inner[ch], first_sign * from_near[0, ch], last_sign * from_near[1, ch]], axis=0)
        high = stack.astype(BF16).astype(F32)
        stack = jnp.concatenate([high, stack - high, high], axis=0).astype(BF16)
        parts = jnp.concatenate(pieces, axis=1) + dot(stack, early[...], ((0,), (0,)))
        return turned_back(parts) + turn[2, :, 0:COLS] * values

    def local_wind(phase):
        for side in range(2):
            near_copy(phase, side).wait()

        def step(i, carry):
            pair = pl.ds(2 * i, 2)
            result = local(phase * PAIRS + i, w[phase, pair].reshape(ITEMS, COLS))
            w[phase, pair] = result.reshape(2, ROWS, COLS)
            return carry

        lax.fori_loop(0, PAIRS, step, 0)

    def grown(ch):
        pltpu.make_async_copy(vr.at[ch], vr.at[ch], vr_sem.at[ch]).wait()
        values = vr[ch]
        high = values.astype(BF16).astype(F32)
        stack = jnp.concatenate([high, values - high, high, jnp.zeros((FAR, 2 * ITEMS), F32)], axis=0).astype(BF16)
        return turned_back(dot(stack, late[...], ((0,), (0,)))).reshape(2, ROWS, COLS)

    x = p // 8
    y = (p // 2) % 4
    core = p % 2
    parity = (x + y) % 2
    busy = polar & ((core == 0) | (parity == 0))
    mine = (2 * core + parity) * PAIRS + 2 * x + y // 2

    def v_copy(to):
        remote = pltpu.make_async_remote_copy(
            src_ref=vs.at[to], dst_ref=vr.at[mine], send_sem=v_sem, recv_sem=vr_sem.at[mine],
            device_id=(z, to), device_id_type=MESH,
        )
        return remote, pltpu.make_async_copy(vs.at[to], vr.at[mine], vr_sem.at[mine])

    @pl.when(polar)
    def _():
        def step(i, carry):
            shrink(2 * PAIRS + i, th[pl.ds(2 * i, 2)].reshape(ITEMS, COLS))
            return carry

        lax.fori_loop(0, PAIRS, step, 0)
        send_u(2)
        for side in range(2):
            near_copy(2, side).start()
        for k in range(5, 9):
            loads[k].wait()
        local_wind(0)

    @pl.when(busy)
    def _():
        pltpu.make_async_copy(zin, zin, z_sem).wait()
        high, low = split(zin[...].reshape(RING * FAR, 2 * ITEMS))
        result = (
            dot(cross[0], high, ((1,), (0,)))
            + dot(cross[0], low, ((1,), (0,)))
            + dot(cross[1], high, ((1,), (0,)))
        )
        vs[...] = result.reshape(RING, FAR, 2 * ITEMS)
        remote, own = v_copy(p)
        own.start()

        for i in range(1, RING):
            remote, own = v_copy((p + i) % RING)
            remote.start()

    @pl.when(polar)
    def _():
        local_wind(1)
        for side in range(2):
            near_copy(2, side).wait()

        def local_thick(i, carry):
            pair = pl.ds(2 * i, 2)
            th[pair] = local(2 * PAIRS + i, th[pair].reshape(ITEMS, COLS)).reshape(2, ROWS, COLS)
            return carry

        lax.fori_loop(0, PAIRS, local_thick, 0)

        def step(i, carry):
            pair = pl.ds(2 * i, 2)
            ext[pair, 0:ROWS, 0:COLS] = th[pair] + grown(2 * PAIRS + i)
            return carry

        lax.fori_loop(0, PAIRS, step, 0)

    @pl.when(jnp.logical_not(polar))
    def _():
        ext[:, 0:ROWS, 0:COLS] = th[...]

    def thick_first(i):
        return ext[2 * i : 2 * i + 2, 0:ROWS, 0:128].reshape(ITEMS, 128)[:, 0:1]

    def thick_last(i):
        return ext[2 * i : 2 * i + 2, 0:ROWS, 256:WIDE].reshape(ITEMS, 128)[:, COLS - 257 : COLS - 256]

    for side, row in ((0, ROWS - 1), (1, 0)):
        for lev in range(LEVELS):
            lat_out[1, side, lev : lev + 1, 0:COLS] = ext[lev, row : row + 1, 0:COLS]
        lat_copy(1, side, (1, BANDS - 1)[side]).start()
    send_lon(1, thick_first, thick_last)

    @pl.when(polar)
    def _():
        for phase in range(2):

            def step(i, carry):
                pair = pl.ds(2 * i, 2)
                w[phase, pair] = w[phase, pair] + grown(phase * PAIRS + i)
                return carry

            lax.fori_loop(0, PAIRS, step, 0)

    wait_edges(1)
    for i in range(PAIRS):
        pair = slice(2 * i, 2 * i + 2)
        tile = ext[pair, 0:ROWS, 256:WIDE].reshape(ITEMS, 128)
        ext[pair, 0:ROWS, 256:WIDE] = with_edges(1, i, tile).reshape(2, ROWS, 128)
    for lev in range(LEVELS):
        ext[lev, ROWS : ROWS + 1] = jnp.where(z == BANDS - 1, 0.0, lat_in[1, 1, lev : lev + 1])
        ext[lev, ROWS + 7 : ROWS + 8] = jnp.where(z == 0, 0.0, lat_in[1, 0, lev : lev + 1])

    @pl.when(polar)
    def _():
        for phase in range(3):
            for t in range(PAIRS):
                to, remote, own = u_copy(phase, t)

                @pl.when(to != p)
                def _():
                    remote.wait_send()

    @pl.when(busy)
    def _():
        def step(i, carry):
            remote, own = v_copy((p + i) % RING)
            remote.wait_send()
            return carry

        lax.fori_loop(1, RING, step, 0)

    @pl.when(jnp.logical_not(polar))
    def _():
        for k in range(4, 9):
            loads[k].wait()


def gradient_kernel(ext_ref, wind_ref, thick_ref, out_ref, geo):
    z, _ = place()
    step = pl.program_id(0)

    @pl.when(step == 0)
    def _():
        geo[...] = press_coef * latitude_tables(z, (ROWS, WIDE))[1]

    for k in range(STEP):
        lev = step * STEP + k
        cells = ext_ref[lev]
        lon_diff = pltpu.roll(cells, WIDE - 1, 1) - pltpu.roll(cells, 1, 1)
        lat_diff = pltpu.roll(cells, ROWS + 7, 0) - pltpu.roll(cells, 1, 0)
        thick_ref[k] = cells[0:ROWS, 0:COLS]
        out_ref[0, k] = wind_ref[0, lev] - (geo[...] * lon_diff[0:ROWS])[:, 0:COLS]
        out_ref[1, k] = wind_ref[1, lev] - (press_coef * lat_diff[0:ROWS])[:, 0:COLS]


def body(thickness, wind, cutoff, tables):
    near, short, early, late, cross = tables
    any_space = pl.BlockSpec(memory_space=pl.ANY)
    dma = pltpu.SemaphoreType.DMA
    ext, moved = pl.pallas_call(
        far_kernel,
        out_shape=(
            pltpu.VMEM((LEVELS, ROWS + 8, WIDE), F32),
            pltpu.VMEM((2, LEVELS, ROWS, COLS), F32),
        ),
        in_specs=[pl.BlockSpec(memory_space=pltpu.HBM)] * 8,
        out_specs=(pl.BlockSpec(memory_space=pltpu.VMEM),) * 2,
        scratch_shapes=[
            pltpu.VMEM((1, 4 * ROWS), jnp.int32),
            pltpu.VMEM((LEVELS, ROWS, COLS), F32),
            pltpu.VMEM((CHUNKS, 2 * ITEMS, 2 * WIDE), BF16),
            pltpu.VMEM((3, ITEMS, WIDE), F32),
            pltpu.VMEM((2, ITEMS, WIDE), F32),
            pltpu.VMEM((ITEMS, WIDE), F32),
            pltpu.VMEM(near.shape, BF16),
            pltpu.VMEM(short.shape, BF16),
            pltpu.VMEM(early.shape, BF16),
            pltpu.VMEM(late.shape, BF16),
            pltpu.VMEM(cross.shape, BF16),
            pltpu.VMEM((CHUNKS, INNER, 2 * ITEMS), F32),
            pltpu.VMEM((2, CHUNKS, NEAR, 2 * ITEMS), F32),
            pltpu.VMEM((2, CHUNKS, NEAR, 2 * ITEMS), F32),
            pltpu.VMEM((CHUNKS, FAR, 2 * ITEMS), F32),
            pltpu.VMEM((RING, FAR, 2 * ITEMS), F32),
            pltpu.VMEM((RING, FAR, 2 * ITEMS), F32),
            pltpu.VMEM((CHUNKS, FAR, 2 * ITEMS), F32),
            pltpu.VMEM((2, ITEMS, 128), F32),
            pltpu.VMEM((2, 2, ITEMS, 128), F32),
            pltpu.VMEM((2, 2, LEVELS, WIDE), F32),
            pltpu.VMEM((2, 2, LEVELS, WIDE), F32),
            dma((9,)),
            dma((3, 2)),
            dma((3, 2)),
            dma,
            dma,
            dma,
            dma((CHUNKS,)),
            dma((2, 2)),
            dma((2, 2)),
            dma((2, 2)),
            dma((2, 2)),
        ],
        compiler_params=pltpu.CompilerParams(
            collective_id=0, has_side_effects=True, vmem_limit_bytes=61865984
        ),
        name="far",
    )(cutoff.reshape(1, -1), thickness, wind, near, short, early, late, cross)
    return pl.pallas_call(
        gradient_kernel,
        grid=(LEVELS // STEP,),
        out_shape=(
            jax.ShapeDtypeStruct((LEVELS, ROWS, COLS), F32),
            jax.ShapeDtypeStruct((2, LEVELS, ROWS, COLS), F32),
        ),
        in_specs=[
            pl.BlockSpec(memory_space=pltpu.VMEM),
            pl.BlockSpec(memory_space=pltpu.VMEM),
        ],
        out_specs=(
            pl.BlockSpec((STEP, ROWS, COLS), lambda i: (i, 0, 0)),
            pl.BlockSpec((2, STEP, ROWS, COLS), lambda i: (0, i, 0, 0)),
        ),
        scratch_shapes=[pltpu.VMEM((ROWS, WIDE), F32)],
        compiler_params=pltpu.CompilerParams(vmem_limit_bytes=40 * 2**20),
        name="gradient",
    )(ext, moved)


def solution(mesh):
    tables = all_tables()
    in_specs = (P(None, "lat", "lon"), P(None, None, "lat", "lon"), P())
    out_specs = (P(None, "lat", "lon"), P(None, None, "lat", "lon"))

    def step(thickness, wind, cutoff):
        return body(thickness, wind, cutoff, tables)

    return jax.shard_map(step, mesh=mesh, in_specs=in_specs, out_specs=out_specs, check_vma=False)
```

```python
import functools
import math

import jax
import jax.numpy as jnp
import numpy as np
from jax import lax
from jax.experimental import pallas as pl
from jax.experimental.pallas import tpu as pltpu
from jax.sharding import PartitionSpec as P

MESH = pl.DeviceIdType.MESH
F32 = jnp.float32
BF16 = jnp.bfloat16

advect_coef = 0.05
press_coef = 0.1
FAR = 8
NEAR = 16
SUB = 128
SUB_RANKS = (13, 22, 13)
INNER = sum(SUB_RANKS)
SHORT = FAR + 2 * NEAR + INNER
SPREAD = INNER + 2 * NEAR
LEVELS = 16
ROWS = 64
COLS = 360
WIDE = 384
BANDS = 8
RING = 32
TOTAL = COLS * RING
PAIRS = LEVELS // 2
CHUNKS = 3 * PAIRS
STEP = 4
TOGETHER = 4
ITEMS = 2 * ROWS


def kernel_block(targets, sources):
    return 1.0 / (TOTAL * np.sin(np.pi * (targets[:, None] - sources[None]) / TOTAL))


def cauchy_tables():
    inside = np.arange(COLS)
    gap = np.arange(SUB)[:, None] - np.arange(SUB)[None]
    diagonal = np.where(gap == 0, 0.0, 1.0 / (TOTAL * np.sin(np.pi * gap / TOTAL) + (gap == 0)))
    far = np.linalg.svd(kernel_block(inside, np.arange(2 * COLS, TOTAL - COLS)), full_matrices=False)[0][:, :FAR]
    cross = np.zeros((RING, FAR, RING, FAR))
    for p in range(RING):
        for q in range(RING):
            if min((p - q) % RING, (q - p) % RING) >= 2:
                cross[p, :, q, :] = far.T @ kernel_block(p * COLS + inside, q * COLS + inside) @ far
    left, scale, right = np.linalg.svd(kernel_block(COLS + inside, inside))
    shorten = [far.T, right[:NEAR], left[:, :NEAR].T]
    from_left = (left * scale)[:, :NEAR].T
    from_right = -(scale[:, None] * right)[:NEAR]
    spread = []
    for k, rank in enumerate(SUB_RANKS):
        own = inside[k * SUB : (k + 1) * SUB]
        other = np.setdiff1d(inside, own)
        rows = np.linalg.svd(kernel_block(other, own), full_matrices=False)[2][:rank]
        padded = np.zeros((rank, COLS))
        padded[:, own] = rows
        shorten.append(padded)
        padded = np.zeros((rank, COLS))
        padded[:, other] = (kernel_block(other, own) @ rows.T).T
        spread.append(padded)
    spread += [from_left, from_right]
    return diagonal, np.concatenate(shorten), np.concatenate(spread), far.T, cross.reshape(RING * FAR, RING * FAR)


def widened(table):
    return np.pad(table, ((0, 0), (0, WIDE - COLS)))


def all_tables():
    diagonal, shorten, spread, far, cross = cauchy_tables()
    high, low = two_parts(diagonal.T)
    near = np.block([[high, low], [high, np.zeros_like(low)]])
    high, low = two_parts(widened(shorten))
    zero = np.zeros((SHORT, SUB), BF16)
    first = [high[:, k : k + SUB] for k in (0, SUB, 2 * SUB)]
    second = [low[:, k : k + SUB] for k in (0, SUB, 2 * SUB)]
    short = np.concatenate(
        [
            np.concatenate([part for f in first for part in (f, f)], axis=1),
            np.concatenate([part for f in second for part in (f, zero)], axis=1),
        ]
    )
    high, low = two_parts(widened(spread))
    early = np.concatenate([high, high, low])
    high, low = two_parts(widened(far))
    late = np.concatenate([high, high, low, np.zeros((FAR, WIDE), BF16)])
    return [jnp.asarray(t) for t in (near, short, early, late, np.stack(two_parts(cross)))]


def two_parts(table):
    table = table.astype(np.float32)
    high = table.astype(BF16)
    low = (table - high.astype(np.float32)).astype(BF16)
    return high, low


def split(values):
    high = values.astype(BF16)
    return high, (values - high.astype(F32)).astype(BF16)


def dot(left, right, dims):
    return lax.dot_general(left, right, (dims, ((), ())), preferred_element_type=F32)


def place():
    z = lax.axis_index("lat")
    p = lax.axis_index("lon")
    return z, p


def latitude_tables(z):
    row = lax.broadcasted_iota(jnp.int32, (ROWS, 128), 0) + z * ROWS
    latitude = math.pi * ((row.astype(F32) + 0.5) / (ROWS * BANDS) - 0.5)
    cosine = jnp.cos(latitude)
    metric = 1.0 / jnp.maximum(cosine, 0.2)
    return [jnp.concatenate([table] * (WIDE // 128), axis=1) for table in (cosine, metric)]


def worker(phase, q):
    x = q // 2
    y = 2 * (q % 2) + (x + phase % 2) % 2
    return x * 8 + y * 2 + phase // 2


def far_kernel(
    cut_hbm, th_hbm, wind_hbm, near_hbm, short_hbm, early_hbm, late_hbm, cross_hbm,
    ext, w,
    cut_ref, th, xs, turn, geo, wide, near, short, early, late, cross,
    inner, to_near, from_near, u, zin, vs, vr,
    lon_out, lon_in, lat_out, lat_in,
    load_sem, near_sem, nearr_sem, u_sem, z_sem, v_sem, vr_sem, lon_sem, lonr_sem, lat_sem, latr_sem,
):
    z, p = place()
    polar = (z < 2) | (z >= 6)
    loads = [
        pltpu.make_async_copy(wind_hbm.at[0], w.at[0], load_sem.at[0]),
        pltpu.make_async_copy(th_hbm, th, load_sem.at[1]),
        pltpu.make_async_copy(wind_hbm.at[1], w.at[1], load_sem.at[2]),
        pltpu.make_async_copy(cut_hbm, cut_ref, load_sem.at[3]),
        pltpu.make_async_copy(short_hbm, short, load_sem.at[4]),
        pltpu.make_async_copy(near_hbm, near, load_sem.at[5]),
        pltpu.make_async_copy(early_hbm, early, load_sem.at[6]),
        pltpu.make_async_copy(cross_hbm, cross, load_sem.at[7]),
        pltpu.make_async_copy(late_hbm, late, load_sem.at[8]),
    ]
    barrier = pltpu.get_barrier_semaphore()

    for k in (3, 0, 1):
        loads[k].start()
    for i in range(1, RING):
        pl.semaphore_signal(barrier, inc=1, device_id=(z, (p + i) % RING), device_id_type=MESH)
    for dz in (1, BANDS - 1):
        pl.semaphore_signal(barrier, inc=1, device_id=((z + dz) % BANDS, p), device_id_type=MESH)
    for k in (2, 4, 5, 6, 7, 8):
        loads[k].start()

    cosine, metric = latitude_tables(z)
    for half in range(2):
        geo[0, half * ROWS : (half + 1) * ROWS] = cosine
        geo[1, half * ROWS : (half + 1) * ROWS] = advect_coef * metric
    wide[...] = jnp.zeros((ITEMS, WIDE), F32)

    loads[3].wait()

    @pl.when(polar)
    def _():
        band = jnp.where(z < 2, z, z - 4)
        row = lax.broadcasted_iota(jnp.int32, (ROWS, 4 * ROWS), 0) + band * ROWS
        lane = lax.broadcasted_iota(jnp.int32, (ROWS, 4 * ROWS), 1)
        cuts = jnp.broadcast_to(cut_ref[...].astype(F32), (ROWS, 4 * ROWS))
        limit = jnp.sum(jnp.where(row == lane, cuts, 0.0), axis=1, keepdims=True)
        odd = 2.0 * limit + 1.0
        column = p * COLS + lax.broadcasted_iota(jnp.int32, (ROWS, WIDE), 1)
        product = jnp.broadcast_to(odd, (ROWS, WIDE)).astype(jnp.int32) * column
        laps = jnp.floor(product.astype(F32) * (0.5 / TOTAL)).astype(jnp.int32)
        angle = (product - laps * (2 * TOTAL)).astype(F32) * (math.pi / TOTAL)
        tables = (jnp.cos(angle), jnp.sin(angle), jnp.broadcast_to(odd * (1.0 / TOTAL), (ROWS, WIDE)))
        for k, table in enumerate(tables):
            for half in range(2):
                turn[k, half * ROWS : (half + 1) * ROWS] = table

        def clear(ch, carry):
            xs[ch, :, 4 * SUB :] = jnp.zeros((2 * ITEMS, 2 * SUB), BF16)
            return carry

        lax.fori_loop(0, CHUNKS, clear, 0)

    pl.semaphore_wait(barrier, RING + 1)

    lane = lax.broadcasted_iota(jnp.int32, (ITEMS, 128), 1)

    def send_lon(kind, first, last):
        edges = jnp.zeros((ITEMS, 128), F32)
        for i in range(PAIRS):
            edges = jnp.where(lane == i, first(i), edges)
            edges = jnp.where(lane == PAIRS + i, last(i), edges)
        lon_out[kind] = edges
        for side, step in ((0, 1), (1, RING - 1)):
            lon_copy(kind, side, step).start()

    def lon_copy(kind, side, step):
        return pltpu.make_async_remote_copy(
            src_ref=lon_out.at[kind], dst_ref=lon_in.at[kind, side],
            send_sem=lon_sem.at[kind, side], recv_sem=lonr_sem.at[kind, side],
            device_id=(z, (p + step) % RING), device_id_type=MESH,
        )

    def lat_copy(kind, side, step):
        return pltpu.make_async_remote_copy(
            src_ref=lat_out.at[kind, side], dst_ref=lat_in.at[kind, side],
            send_sem=lat_sem.at[kind, side], recv_sem=latr_sem.at[kind, side],
            device_id=((z + step) % BANDS, p), device_id_type=MESH,
        )

    def wait_edges(kind):
        for side, step in ((0, 1), (1, RING - 1)):
            lon_copy(kind, side, step).wait()
        for side, step in ((0, 1), (1, BANDS - 1)):
            lat_copy(kind, side, step).wait()

    def with_edges(kind, i, tile):
        left = lon_in[kind, 0, :, PAIRS + i : PAIRS + i + 1]
        right = lon_in[kind, 1, :, i : i + 1]
        return jnp.where(lane == COLS - 256, right, jnp.where(lane == 127, left, tile))

    loads[0].wait()
    loads[1].wait()

    def flux_first(i):
        return (th[2 * i : 2 * i + 2, :, 0:128] * w[0, 2 * i : 2 * i + 2, :, 0:128]).reshape(ITEMS, 128)[:, 0:1]

    def flux_last(i):
        tile = th[2 * i : 2 * i + 2, :, 256:COLS] * w[0, 2 * i : 2 * i + 2, :, 256:COLS]
        return tile.reshape(ITEMS, COLS - 256)[:, COLS - 257 : COLS - 256]

    send_lon(0, flux_first, flux_last)
    loads[2].wait()
    for side, row in ((0, ROWS - 1), (1, 0)):
        for lev in range(LEVELS):
            lat_out[0, side, lev : lev + 1, 0:COLS] = (
                th[lev, row : row + 1] * w[1, lev, row : row + 1] * geo[0, row : row + 1, 0:COLS]
            )
        lat_copy(0, side, (1, BANDS - 1)[side]).start()

    def several(work):
        def step(i, carry):
            work([TOGETHER * i + k for k in range(TOGETHER)])
            return carry

        lax.fori_loop(0, PAIRS // TOGETHER, step, 0)

    def shrink(chunks, values):
        for ch, part in zip(chunks, values):
            widen(ch, part)
        for ch in chunks:
            shorten(ch)

    def widen(ch, values):
        for half in range(2):
            rows = slice(half * ITEMS, (half + 1) * ITEMS)
            high, low = split(values * turn[half, :, 0:COLS])
            for k in range(3):
                size = min(SUB, COLS - k * SUB)
                xs[ch, rows, 2 * k * SUB : 2 * k * SUB + size] = high[:, k * SUB : k * SUB + size]
                xs[ch, rows, (2 * k + 1) * SUB : (2 * k + 1) * SUB + size] = low[:, k * SUB : k * SUB + size]

    def shorten(ch):
        both = dot(short[...], xs[ch], ((1,), (1,)))
        both = both[0:SHORT] + both[SHORT:]
        u[ch] = both[0:FAR]
        to_near[0, ch] = both[FAR : FAR + NEAR]
        to_near[1, ch] = both[FAR + NEAR : FAR + 2 * NEAR]
        inner[ch] = both[FAR + 2 * NEAR :]

    def near_copy(phase, side):
        part = pl.ds(phase * PAIRS, PAIRS)
        return pltpu.make_async_remote_copy(
            src_ref=to_near.at[side, part], dst_ref=from_near.at[side, part],
            send_sem=near_sem.at[phase, side], recv_sem=nearr_sem.at[phase, side],
            device_id=(z, (p + (1, RING - 1)[side]) % RING), device_id_type=MESH,
        )

    def u_copy(phase, t):
        q = (t + p) % PAIRS
        ch = phase * PAIRS + q
        to = worker(phase, q)
        remote = pltpu.make_async_remote_copy(
            src_ref=u.at[ch], dst_ref=zin.at[p], send_sem=u_sem, recv_sem=z_sem,
            device_id=(z, to), device_id_type=MESH,
        )
        return to, remote, pltpu.make_async_copy(u.at[ch], zin.at[p], z_sem)

    def send_u(phase):
        for t in range(PAIRS):
            to, remote, own = u_copy(phase, t)

            @pl.when(to != p)
            def _():
                remote.start()

            @pl.when(to == p)
            def _():
                own.start()

    @pl.when(polar)
    def _():
        loads[4].wait()
        for phase in range(2):

            several(
                lambda parts: shrink(
                    [phase * PAIRS + i for i in parts],
                    [w[phase, pl.ds(2 * i, 2)].reshape(ITEMS, COLS) for i in parts],
                )
            )
            send_u(phase)
            for side in range(2):
                near_copy(phase, side).start()

    row_index = lax.broadcasted_iota(jnp.int32, (ROWS, WIDE), 0)
    for i in range(PAIRS):
        pair = slice(2 * i, 2 * i + 2)
        wide[:, 0:COLS] = (th[pair] * w[0, pair]).reshape(ITEMS, COLS)
        flux = wide[...]
        lon_diff = pltpu.roll(flux, WIDE - 1, 1) - pltpu.roll(flux, 1, 1)
        wide[:, 0:COLS] = (th[pair] * w[1, pair]).reshape(ITEMS, COLS)
        flux = wide[...] * geo[0]
        for k in range(2):
            lev = 2 * i + k
            cells = flux[k * ROWS : (k + 1) * ROWS]
            up = jnp.where(row_index == ROWS - 1, 0.0, pltpu.roll(cells, ROWS - 1, 0))
            down = jnp.where(row_index == 0, 0.0, pltpu.roll(cells, 1, 0))
            change = geo[1, 0:ROWS] * (lon_diff[k * ROWS : (k + 1) * ROWS] + (up - down))
            th[lev] = th[lev] - change[:, 0:COLS]
    wait_edges(0)
    last_lane = lax.broadcasted_iota(jnp.int32, (ITEMS, COLS - 256), 1)
    for i in range(PAIRS):
        pair = slice(2 * i, 2 * i + 2)
        left = lon_in[0, 0, :, PAIRS + i : PAIRS + i + 1] * geo[1, :, 0:128]
        right = lon_in[0, 1, :, i : i + 1] * geo[1, :, 0 : COLS - 256]
        tile = th[pair, :, 0:128].reshape(ITEMS, 128)
        th[pair, :, 0:128] = jnp.where(lane == 0, tile + left, tile).reshape(2, ROWS, 128)
        tile = th[pair, :, 256:COLS].reshape(ITEMS, COLS - 256)
        tile = jnp.where(last_lane == COLS - 257, tile - right, tile)
        th[pair, :, 256:COLS] = tile.reshape(2, ROWS, COLS - 256)
    for lev in range(LEVELS):
        south = jnp.where(z == 0, 0.0, lat_in[0, 0, lev : lev + 1, 0:COLS])
        north = jnp.where(z == BANDS - 1, 0.0, lat_in[0, 1, lev : lev + 1, 0:COLS])
        th[lev, 0:1] = th[lev, 0:1] + geo[1, 0:1, 0:COLS] * south
        th[lev, ROWS - 1 : ROWS] = th[lev, ROWS - 1 : ROWS] - geo[1, ROWS - 1 : ROWS, 0:COLS] * north

    first_sign = jnp.where(p == 0, -1.0, 1.0).astype(F32)
    last_sign = jnp.where(p == RING - 1, -1.0, 1.0).astype(F32)

    def turned_back(parts):
        mixed = turn[1] * parts[0:ITEMS] - turn[0] * parts[ITEMS:]
        return mixed[:, 0:COLS]

    def local(ch, values):
        pieces = []
        for k in range(3):
            both = dot(xs[ch, :, 2 * k * SUB : (2 * k + 2) * SUB], near[...], ((1,), (0,)))
            pieces.append(both[:, 0:SUB] + both[:, SUB:])
        stack = jnp.concatenate([inner[ch], first_sign * from_near[0, ch], last_sign * from_near[1, ch]], axis=0)
        high = stack.astype(BF16).astype(F32)
        stack = jnp.concatenate([high, stack - high, high], axis=0).astype(BF16)
        parts = jnp.concatenate(pieces, axis=1) + dot(stack, early[...], ((0,), (0,)))
        return turned_back(parts) + turn[2, :, 0:COLS] * values

    def local_wind(phase):
        for side in range(2):
            near_copy(phase, side).wait()

        def work(parts):
            pairs = [pl.ds(2 * i, 2) for i in parts]
            results = [
                local(phase * PAIRS + i, w[phase, pair].reshape(ITEMS, COLS)) for i, pair in zip(parts, pairs)
            ]
            for pair, result in zip(pairs, results):
                w[phase, pair] = result.reshape(2, ROWS, COLS)

        several(work)

    def arrived(chunks):
        for ch in chunks:
            pltpu.make_async_copy(vr.at[ch], vr.at[ch], vr_sem.at[ch]).wait()

    def grown(ch):
        values = vr[ch]
        high = values.astype(BF16).astype(F32)
        stack = jnp.concatenate([high, values - high, high, jnp.zeros((FAR, 2 * ITEMS), F32)], axis=0).astype(BF16)
        return turned_back(dot(stack, late[...], ((0,), (0,)))).reshape(2, ROWS, COLS)

    x = p // 8
    y = (p // 2) % 4
    core = p % 2
    parity = (x + y) % 2
    busy = polar & ((core == 0) | (parity == 0))
    mine = (2 * core + parity) * PAIRS + 2 * x + y // 2

    def v_copy(to):
        remote = pltpu.make_async_remote_copy(
            src_ref=vs.at[to], dst_ref=vr.at[mine], send_sem=v_sem, recv_sem=vr_sem.at[mine],
            device_id=(z, to), device_id_type=MESH,
        )
        return remote, pltpu.make_async_copy(vs.at[to], vr.at[mine], vr_sem.at[mine])

    @pl.when(polar)
    def _():
        several(
            lambda parts: shrink(
                [2 * PAIRS + i for i in parts],
                [th[pl.ds(2 * i, 2)].reshape(ITEMS, COLS) for i in parts],
            )
        )
        send_u(2)
        for side in range(2):
            near_copy(2, side).start()
        for k in range(5, 9):
            loads[k].wait()
        local_wind(0)

    @pl.when(busy)
    def _():
        pltpu.make_async_copy(zin, zin, z_sem).wait()
        high, low = split(zin[...].reshape(RING * FAR, 2 * ITEMS))
        result = (
            dot(cross[0], high, ((1,), (0,)))
            + dot(cross[0], low, ((1,), (0,)))
            + dot(cross[1], high, ((1,), (0,)))
        )
        vs[...] = result.reshape(RING, FAR, 2 * ITEMS)
        remote, own = v_copy(p)
        own.start()

        for i in range(1, RING):
            remote, own = v_copy((p + i) % RING)
            remote.start()

    @pl.when(polar)
    def _():
        for side in range(2):
            near_copy(2, side).wait()

        def local_thick(parts):
            pairs = [pl.ds(2 * i, 2) for i in parts]
            results = [local(2 * PAIRS + i, th[pair].reshape(ITEMS, COLS)) for i, pair in zip(parts, pairs)]
            for pair, result in zip(pairs, results):
                th[pair] = result.reshape(2, ROWS, COLS)

        several(local_thick)

        def work(parts):
            arrived([2 * PAIRS + i for i in parts])
            pairs = [pl.ds(2 * i, 2) for i in parts]
            results = [th[pair] + grown(2 * PAIRS + i) for i, pair in zip(parts, pairs)]
            for pair, result in zip(pairs, results):
                ext[pair, 0:ROWS, 0:COLS] = result

        several(work)

    @pl.when(jnp.logical_not(polar))
    def _():
        ext[:, 0:ROWS, 0:COLS] = th[...]

    def thick_first(i):
        return ext[2 * i : 2 * i + 2, 0:ROWS, 0:128].reshape(ITEMS, 128)[:, 0:1]

    def thick_last(i):
        return ext[2 * i : 2 * i + 2, 0:ROWS, 256:WIDE].reshape(ITEMS, 128)[:, COLS - 257 : COLS - 256]

    for side, row in ((0, ROWS - 1), (1, 0)):
        for lev in range(LEVELS):
            lat_out[1, side, lev : lev + 1, 0:COLS] = ext[lev, row : row + 1, 0:COLS]
        lat_copy(1, side, (1, BANDS - 1)[side]).start()
    send_lon(1, thick_first, thick_last)

    @pl.when(polar)
    def _():
        local_wind(1)
        for phase in range(2):

            def work(parts):
                arrived([phase * PAIRS + i for i in parts])
                pairs = [pl.ds(2 * i, 2) for i in parts]
                results = [w[phase, pair] + grown(phase * PAIRS + i) for i, pair in zip(parts, pairs)]
                for pair, result in zip(pairs, results):
                    w[phase, pair] = result

            several(work)

    wait_edges(1)
    for i in range(PAIRS):
        pair = slice(2 * i, 2 * i + 2)
        tile = ext[pair, 0:ROWS, 256:WIDE].reshape(ITEMS, 128)
        ext[pair, 0:ROWS, 256:WIDE] = with_edges(1, i, tile).reshape(2, ROWS, 128)
    for lev in range(LEVELS):
        ext[lev, ROWS : ROWS + 1] = jnp.where(z == BANDS - 1, 0.0, lat_in[1, 1, lev : lev + 1])
        ext[lev, ROWS + 7 : ROWS + 8] = jnp.where(z == 0, 0.0, lat_in[1, 0, lev : lev + 1])

    @pl.when(polar)
    def _():
        for phase in range(3):
            for t in range(PAIRS):
                to, remote, own = u_copy(phase, t)

                @pl.when(to != p)
                def _():
                    remote.wait_send()

    @pl.when(busy)
    def _():
        def step(i, carry):
            remote, own = v_copy((p + i) % RING)
            remote.wait_send()
            return carry

        lax.fori_loop(1, RING, step, 0)

    @pl.when(jnp.logical_not(polar))
    def _():
        for k in range(4, 9):
            loads[k].wait()


def gradient_kernel(ext_ref, wind_ref, thick_ref, out_ref, geo):
    z, _ = place()
    step = pl.program_id(0)

    @pl.when(step == 0)
    def _():
        geo[...] = press_coef * latitude_tables(z)[1]

    for k in range(STEP):
        lev = step * STEP + k
        cells = ext_ref[lev]
        lon_diff = pltpu.roll(cells, WIDE - 1, 1) - pltpu.roll(cells, 1, 1)
        lat_diff = pltpu.roll(cells, ROWS + 7, 0) - pltpu.roll(cells, 1, 0)
        thick_ref[k] = cells[0:ROWS, 0:COLS]
        out_ref[0, k] = wind_ref[0, lev] - (geo[...] * lon_diff[0:ROWS])[:, 0:COLS]
        out_ref[1, k] = wind_ref[1, lev] - (press_coef * lat_diff[0:ROWS])[:, 0:COLS]


def body(thickness, wind, cutoff, tables):
    near, short, early, late, cross = tables
    any_space = pl.BlockSpec(memory_space=pl.ANY)
    dma = pltpu.SemaphoreType.DMA
    ext, moved = pl.pallas_call(
        far_kernel,
        out_shape=(
            pltpu.VMEM((LEVELS, ROWS + 8, WIDE), F32),
            pltpu.VMEM((2, LEVELS, ROWS, COLS), F32),
        ),
        in_specs=[pl.BlockSpec(memory_space=pltpu.HBM)] * 8,
        out_specs=(pl.BlockSpec(memory_space=pltpu.VMEM),) * 2,
        scratch_shapes=[
            pltpu.VMEM((1, 4 * ROWS), jnp.int32),
            pltpu.VMEM((LEVELS, ROWS, COLS), F32),
            pltpu.VMEM((CHUNKS, 2 * ITEMS, 2 * WIDE), BF16),
            pltpu.VMEM((3, ITEMS, WIDE), F32),
            pltpu.VMEM((2, ITEMS, WIDE), F32),
            pltpu.VMEM((ITEMS, WIDE), F32),
            pltpu.VMEM(near.shape, BF16),
            pltpu.VMEM(short.shape, BF16),
            pltpu.VMEM(early.shape, BF16),
            pltpu.VMEM(late.shape, BF16),
            pltpu.VMEM(cross.shape, BF16),
            pltpu.VMEM((CHUNKS, INNER, 2 * ITEMS), F32),
            pltpu.VMEM((2, CHUNKS, NEAR, 2 * ITEMS), F32),
            pltpu.VMEM((2, CHUNKS, NEAR, 2 * ITEMS), F32),
            pltpu.VMEM((CHUNKS, FAR, 2 * ITEMS), F32),
            pltpu.VMEM((RING, FAR, 2 * ITEMS), F32),
            pltpu.VMEM((RING, FAR, 2 * ITEMS), F32),
            pltpu.VMEM((CHUNKS, FAR, 2 * ITEMS), F32),
            pltpu.VMEM((2, ITEMS, 128), F32),
            pltpu.VMEM((2, 2, ITEMS, 128), F32),
            pltpu.VMEM((2, 2, LEVELS, WIDE), F32),
            pltpu.VMEM((2, 2, LEVELS, WIDE), F32),
            dma((9,)),
            dma((3, 2)),
            dma((3, 2)),
            dma,
            dma,
            dma,
            dma((CHUNKS,)),
            dma((2, 2)),
            dma((2, 2)),
            dma((2, 2)),
            dma((2, 2)),
        ],
        compiler_params=pltpu.CompilerParams(
            collective_id=0, has_side_effects=True, vmem_limit_bytes=61865984
        ),
        name="far",
    )(cutoff.reshape(1, -1), thickness, wind, near, short, early, late, cross)
    return pl.pallas_call(
        gradient_kernel,
        grid=(LEVELS // STEP,),
        out_shape=(
            jax.ShapeDtypeStruct((LEVELS, ROWS, COLS), F32),
            jax.ShapeDtypeStruct((2, LEVELS, ROWS, COLS), F32),
        ),
        in_specs=[
            pl.BlockSpec(memory_space=pltpu.VMEM),
            pl.BlockSpec(memory_space=pltpu.VMEM),
        ],
        out_specs=(
            pl.BlockSpec((STEP, ROWS, COLS), lambda i: (i, 0, 0)),
            pl.BlockSpec((2, STEP, ROWS, COLS), lambda i: (0, i, 0, 0)),
        ),
        scratch_shapes=[pltpu.VMEM((ROWS, WIDE), F32)],
        compiler_params=pltpu.CompilerParams(vmem_limit_bytes=40 * 2**20),
        name="gradient",
    )(ext, moved)


def solution(mesh):
    tables = all_tables()
    in_specs = (P(None, "lat", "lon"), P(None, None, "lat", "lon"), P())
    out_specs = (P(None, "lat", "lon"), P(None, None, "lat", "lon"))

    def step(thickness, wind, cutoff):
        return body(thickness, wind, cutoff, tables)

    return jax.shard_map(step, mesh=mesh, in_specs=in_specs, out_specs=out_specs, check_vma=False)
```

```python
import functools
import math

import jax
import jax.numpy as jnp
import numpy as np
from jax import lax
from jax.experimental import pallas as pl
from jax.experimental.pallas import tpu as pltpu
from jax.sharding import PartitionSpec as P

MESH = pl.DeviceIdType.MESH
F32 = jnp.float32
BF16 = jnp.bfloat16

advect_coef = 0.05
press_coef = 0.1
FAR = 8
NEAR = 16
SUB = 128
SUB_RANKS = (13, 22, 13)
INNER = sum(SUB_RANKS)
SHORT = FAR + 2 * NEAR + INNER
SPREAD = INNER + 2 * NEAR
LEVELS = 16
ROWS = 64
COLS = 360
WIDE = 384
BANDS = 8
RING = 32
TOTAL = COLS * RING
PAIRS = LEVELS // 2
CHUNKS = 3 * PAIRS
STEP = 4
TOGETHER = 4
ITEMS = 2 * ROWS


def kernel_block(targets, sources):
    return 1.0 / (TOTAL * np.sin(np.pi * (targets[:, None] - sources[None]) / TOTAL))


def cauchy_tables():
    inside = np.arange(COLS)
    gap = np.arange(SUB)[:, None] - np.arange(SUB)[None]
    diagonal = np.where(gap == 0, 0.0, 1.0 / (TOTAL * np.sin(np.pi * gap / TOTAL) + (gap == 0)))
    far = np.linalg.svd(kernel_block(inside, np.arange(2 * COLS, TOTAL - COLS)), full_matrices=False)[0][:, :FAR]
    cross = np.zeros((RING, FAR, RING, FAR))
    for p in range(RING):
        for q in range(RING):
            if min((p - q) % RING, (q - p) % RING) >= 2:
                cross[p, :, q, :] = far.T @ kernel_block(p * COLS + inside, q * COLS + inside) @ far
    left, scale, right = np.linalg.svd(kernel_block(COLS + inside, inside))
    shorten = [far.T, right[:NEAR], left[:, :NEAR].T]
    from_left = (left * scale)[:, :NEAR].T
    from_right = -(scale[:, None] * right)[:NEAR]
    spread = []
    for k, rank in enumerate(SUB_RANKS):
        own = inside[k * SUB : (k + 1) * SUB]
        other = np.setdiff1d(inside, own)
        rows = np.linalg.svd(kernel_block(other, own), full_matrices=False)[2][:rank]
        padded = np.zeros((rank, COLS))
        padded[:, own] = rows
        shorten.append(padded)
        padded = np.zeros((rank, COLS))
        padded[:, other] = (kernel_block(other, own) @ rows.T).T
        spread.append(padded)
    spread += [from_left, from_right]
    return diagonal, np.concatenate(shorten), np.concatenate(spread), far.T, cross.reshape(RING * FAR, RING * FAR)


def widened(table):
    return np.pad(table, ((0, 0), (0, WIDE - COLS)))


def all_tables():
    diagonal, shorten, spread, far, cross = cauchy_tables()
    high, low = two_parts(diagonal.T)
    near = np.block([[high, low], [high, np.zeros_like(low)]])
    high, low = two_parts(widened(shorten))
    zero = np.zeros((SHORT, SUB), BF16)
    first = [high[:, k : k + SUB] for k in (0, SUB, 2 * SUB)]
    second = [low[:, k : k + SUB] for k in (0, SUB, 2 * SUB)]
    short = np.concatenate(
        [
            np.concatenate([part for f in first for part in (f, f)], axis=1),
            np.concatenate([part for f in second for part in (f, zero)], axis=1),
        ]
    )
    high, low = two_parts(widened(spread))
    early = np.concatenate([high, high, low])
    high, low = two_parts(widened(far))
    late = np.concatenate([high, high, low, np.zeros((FAR, WIDE), BF16)])
    return [jnp.asarray(t) for t in (near, short, early, late, np.stack(two_parts(cross)))]


def two_parts(table):
    table = table.astype(np.float32)
    high = table.astype(BF16)
    low = (table - high.astype(np.float32)).astype(BF16)
    return high, low


def split(values):
    high = values.astype(BF16)
    return high, (values - high.astype(F32)).astype(BF16)


def dot(left, right, dims):
    return lax.dot_general(left, right, (dims, ((), ())), preferred_element_type=F32)


def place():
    z = lax.axis_index("lat")
    p = lax.axis_index("lon")
    return z, p


def latitude_tables(z):
    row = lax.broadcasted_iota(jnp.int32, (ROWS, 128), 0) + z * ROWS
    latitude = math.pi * ((row.astype(F32) + 0.5) / (ROWS * BANDS) - 0.5)
    cosine = jnp.cos(latitude)
    metric = 1.0 / jnp.maximum(cosine, 0.2)
    return [jnp.concatenate([table] * (WIDE // 128), axis=1) for table in (cosine, metric)]


def worker(phase, q):
    x = q // 2
    y = 2 * (q % 2) + (x + phase % 2) % 2
    return x * 8 + y * 2 + phase // 2


def far_kernel(
    cut_hbm, th_hbm, wind_hbm, near_hbm, short_hbm, early_hbm, late_hbm, cross_hbm,
    ext, w,
    cut_ref, th, xs, turn, geo, wide, near, short, early, late, cross,
    inner, to_near, from_near, u, zin, vs, vr,
    lon_out, lon_in, lat_out, lat_in,
    load_sem, near_sem, nearr_sem, u_sem, z_sem, v_sem, vr_sem, lon_sem, lonr_sem, lat_sem, latr_sem,
):
    z, p = place()
    polar = (z < 2) | (z >= 6)
    loads = [
        pltpu.make_async_copy(wind_hbm.at[0], w.at[0], load_sem.at[0]),
        pltpu.make_async_copy(th_hbm, th, load_sem.at[1]),
        pltpu.make_async_copy(wind_hbm.at[1], w.at[1], load_sem.at[2]),
        pltpu.make_async_copy(cut_hbm, cut_ref, load_sem.at[3]),
        pltpu.make_async_copy(short_hbm, short, load_sem.at[4]),
        pltpu.make_async_copy(near_hbm, near, load_sem.at[5]),
        pltpu.make_async_copy(early_hbm, early, load_sem.at[6]),
        pltpu.make_async_copy(cross_hbm, cross, load_sem.at[7]),
        pltpu.make_async_copy(late_hbm, late, load_sem.at[8]),
    ]
    barrier = pltpu.get_barrier_semaphore()

    for k in (3, 0, 1):
        loads[k].start()
    for i in range(1, RING):
        pl.semaphore_signal(barrier, inc=1, device_id=(z, (p + i) % RING), device_id_type=MESH)
    for dz in (1, BANDS - 1):
        pl.semaphore_signal(barrier, inc=1, device_id=((z + dz) % BANDS, p), device_id_type=MESH)
    for k in (2, 4, 5, 6, 7, 8):
        loads[k].start()

    cosine, metric = latitude_tables(z)
    for half in range(2):
        geo[0, half * ROWS : (half + 1) * ROWS] = cosine
        geo[1, half * ROWS : (half + 1) * ROWS] = advect_coef * metric
    wide[...] = jnp.zeros((4, ITEMS, WIDE), F32)

    loads[3].wait()

    @pl.when(polar)
    def _():
        band = jnp.where(z < 2, z, z - 4)
        row = lax.broadcasted_iota(jnp.int32, (ROWS, 4 * ROWS), 0) + band * ROWS
        lane = lax.broadcasted_iota(jnp.int32, (ROWS, 4 * ROWS), 1)
        cuts = jnp.broadcast_to(cut_ref[...].astype(F32), (ROWS, 4 * ROWS))
        limit = jnp.sum(jnp.where(row == lane, cuts, 0.0), axis=1, keepdims=True)
        odd = 2.0 * limit + 1.0
        column = p * COLS + lax.broadcasted_iota(jnp.int32, (ROWS, WIDE), 1)
        product = jnp.broadcast_to(odd, (ROWS, WIDE)).astype(jnp.int32) * column
        laps = jnp.floor(product.astype(F32) * (0.5 / TOTAL)).astype(jnp.int32)
        angle = (product - laps * (2 * TOTAL)).astype(F32) * (math.pi / TOTAL)
        tables = (jnp.cos(angle), jnp.sin(angle), jnp.broadcast_to(odd * (1.0 / TOTAL), (ROWS, WIDE)))
        for k, table in enumerate(tables):
            for half in range(2):
                turn[k, half * ROWS : (half + 1) * ROWS] = table

        def clear(ch, carry):
            xs[ch, :, 4 * SUB :] = jnp.zeros((2 * ITEMS, 2 * SUB), BF16)
            return carry

        lax.fori_loop(0, CHUNKS, clear, 0)

    pl.semaphore_wait(barrier, RING + 1)

    lane = lax.broadcasted_iota(jnp.int32, (ITEMS, 128), 1)

    def send_lon(kind, first, last):
        edges = jnp.zeros((ITEMS, 128), F32)
        for i in range(PAIRS):
            edges = jnp.where(lane == i, first(i), edges)
            edges = jnp.where(lane == PAIRS + i, last(i), edges)
        lon_out[kind] = edges
        for side, step in ((0, 1), (1, RING - 1)):
            lon_copy(kind, side, step).start()

    def lon_copy(kind, side, step):
        return pltpu.make_async_remote_copy(
            src_ref=lon_out.at[kind], dst_ref=lon_in.at[kind, side],
            send_sem=lon_sem.at[kind, side], recv_sem=lonr_sem.at[kind, side],
            device_id=(z, (p + step) % RING), device_id_type=MESH,
        )

    def lat_copy(kind, side, step):
        return pltpu.make_async_remote_copy(
            src_ref=lat_out.at[kind, side], dst_ref=lat_in.at[kind, side],
            send_sem=lat_sem.at[kind, side], recv_sem=latr_sem.at[kind, side],
            device_id=((z + step) % BANDS, p), device_id_type=MESH,
        )

    def wait_edges(kind):
        for side, step in ((0, 1), (1, RING - 1)):
            lon_copy(kind, side, step).wait()
        for side, step in ((0, 1), (1, BANDS - 1)):
            lat_copy(kind, side, step).wait()

    def with_edges(kind, i, tile):
        left = lon_in[kind, 0, :, PAIRS + i : PAIRS + i + 1]
        right = lon_in[kind, 1, :, i : i + 1]
        return jnp.where(lane == COLS - 256, right, jnp.where(lane == 127, left, tile))

    loads[0].wait()
    loads[1].wait()

    def flux_first(i):
        return (th[2 * i : 2 * i + 2, :, 0:128] * w[0, 2 * i : 2 * i + 2, :, 0:128]).reshape(ITEMS, 128)[:, 0:1]

    def flux_last(i):
        tile = th[2 * i : 2 * i + 2, :, 256:COLS] * w[0, 2 * i : 2 * i + 2, :, 256:COLS]
        return tile.reshape(ITEMS, COLS - 256)[:, COLS - 257 : COLS - 256]

    send_lon(0, flux_first, flux_last)
    loads[2].wait()
    for side, row in ((0, ROWS - 1), (1, 0)):
        for lev in range(LEVELS):
            lat_out[0, side, lev : lev + 1, 0:COLS] = (
                th[lev, row : row + 1] * w[1, lev, row : row + 1] * geo[0, row : row + 1, 0:COLS]
            )
        lat_copy(0, side, (1, BANDS - 1)[side]).start()

    def several(work):
        def step(i, carry):
            work([TOGETHER * i + k for k in range(TOGETHER)])
            return carry

        lax.fori_loop(0, PAIRS // TOGETHER, step, 0)

    def shrink(chunks, values):
        for ch, part in zip(chunks, values):
            widen(ch, part)
        for ch in chunks:
            shorten(ch)

    def widen(ch, values):
        for half in range(2):
            rows = slice(half * ITEMS, (half + 1) * ITEMS)
            high, low = split(values * turn[half, :, 0:COLS])
            for k in range(3):
                size = min(SUB, COLS - k * SUB)
                xs[ch, rows, 2 * k * SUB : 2 * k * SUB + size] = high[:, k * SUB : k * SUB + size]
                xs[ch, rows, (2 * k + 1) * SUB : (2 * k + 1) * SUB + size] = low[:, k * SUB : k * SUB + size]

    def shorten(ch):
        both = dot(short[...], xs[ch], ((1,), (1,)))
        both = both[0:SHORT] + both[SHORT:]
        u[ch] = both[0:FAR]
        to_near[0, ch] = both[FAR : FAR + NEAR]
        to_near[1, ch] = both[FAR + NEAR : FAR + 2 * NEAR]
        inner[ch] = both[FAR + 2 * NEAR :]

    def near_copy(phase, side):
        part = pl.ds(phase * PAIRS, PAIRS)
        return pltpu.make_async_remote_copy(
            src_ref=to_near.at[side, part], dst_ref=from_near.at[side, part],
            send_sem=near_sem.at[phase, side], recv_sem=nearr_sem.at[phase, side],
            device_id=(z, (p + (1, RING - 1)[side]) % RING), device_id_type=MESH,
        )

    def u_copy(phase, t):
        q = (t + p) % PAIRS
        ch = phase * PAIRS + q
        to = worker(phase, q)
        remote = pltpu.make_async_remote_copy(
            src_ref=u.at[ch], dst_ref=zin.at[p], send_sem=u_sem, recv_sem=z_sem,
            device_id=(z, to), device_id_type=MESH,
        )
        return to, remote, pltpu.make_async_copy(u.at[ch], zin.at[p], z_sem)

    def send_u(phase):
        for t in range(PAIRS):
            to, remote, own = u_copy(phase, t)

            @pl.when(to != p)
            def _():
                remote.start()

            @pl.when(to == p)
            def _():
                own.start()

    @pl.when(polar)
    def _():
        loads[4].wait()
        for phase in range(2):

            several(
                lambda parts: shrink(
                    [phase * PAIRS + i for i in parts],
                    [w[phase, pl.ds(2 * i, 2)].reshape(ITEMS, COLS) for i in parts],
                )
            )
            send_u(phase)
            for side in range(2):
                near_copy(phase, side).start()

    row_index = lax.broadcasted_iota(jnp.int32, (ROWS, WIDE), 0)
    for i in range(PAIRS):
        pair = slice(2 * i, 2 * i + 2)
        first, second = 2 * (i % 2), 2 * (i % 2) + 1
        wide[first, :, 0:COLS] = (th[pair] * w[0, pair]).reshape(ITEMS, COLS)
        wide[second, :, 0:COLS] = (th[pair] * w[1, pair]).reshape(ITEMS, COLS)
        flux = wide[first]
        lon_diff = pltpu.roll(flux, WIDE - 1, 1) - pltpu.roll(flux, 1, 1)
        flux = wide[second] * geo[0]
        for k in range(2):
            lev = 2 * i + k
            cells = flux[k * ROWS : (k + 1) * ROWS]
            up = jnp.where(row_index == ROWS - 1, 0.0, pltpu.roll(cells, ROWS - 1, 0))
            down = jnp.where(row_index == 0, 0.0, pltpu.roll(cells, 1, 0))
            change = geo[1, 0:ROWS] * (lon_diff[k * ROWS : (k + 1) * ROWS] + (up - down))
            th[lev] = th[lev] - change[:, 0:COLS]
    wait_edges(0)
    last_lane = lax.broadcasted_iota(jnp.int32, (ITEMS, COLS - 256), 1)
    for i in range(PAIRS):
        pair = slice(2 * i, 2 * i + 2)
        left = lon_in[0, 0, :, PAIRS + i : PAIRS + i + 1] * geo[1, :, 0:128]
        right = lon_in[0, 1, :, i : i + 1] * geo[1, :, 0 : COLS - 256]
        tile = th[pair, :, 0:128].reshape(ITEMS, 128)
        th[pair, :, 0:128] = jnp.where(lane == 0, tile + left, tile).reshape(2, ROWS, 128)
        tile = th[pair, :, 256:COLS].reshape(ITEMS, COLS - 256)
        tile = jnp.where(last_lane == COLS - 257, tile - right, tile)
        th[pair, :, 256:COLS] = tile.reshape(2, ROWS, COLS - 256)
    for lev in range(LEVELS):
        south = jnp.where(z == 0, 0.0, lat_in[0, 0, lev : lev + 1, 0:COLS])
        north = jnp.where(z == BANDS - 1, 0.0, lat_in[0, 1, lev : lev + 1, 0:COLS])
        th[lev, 0:1] = th[lev, 0:1] + geo[1, 0:1, 0:COLS] * south
        th[lev, ROWS - 1 : ROWS] = th[lev, ROWS - 1 : ROWS] - geo[1, ROWS - 1 : ROWS, 0:COLS] * north

    first_sign = jnp.where(p == 0, -1.0, 1.0).astype(F32)
    last_sign = jnp.where(p == RING - 1, -1.0, 1.0).astype(F32)

    def turned_back(parts):
        mixed = turn[1] * parts[0:ITEMS] - turn[0] * parts[ITEMS:]
        return mixed[:, 0:COLS]

    def local(ch, values):
        pieces = []
        for k in range(3):
            both = dot(xs[ch, :, 2 * k * SUB : (2 * k + 2) * SUB], near[...], ((1,), (0,)))
            pieces.append(both[:, 0:SUB] + both[:, SUB:])
        stack = jnp.concatenate([inner[ch], first_sign * from_near[0, ch], last_sign * from_near[1, ch]], axis=0)
        high = stack.astype(BF16).astype(F32)
        stack = jnp.concatenate([high, stack - high, high], axis=0).astype(BF16)
        parts = jnp.concatenate(pieces, axis=1) + dot(stack, early[...], ((0,), (0,)))
        return turned_back(parts) + turn[2, :, 0:COLS] * values

    def local_wind(phase):
        for side in range(2):
            near_copy(phase, side).wait()

        def work(parts):
            pairs = [pl.ds(2 * i, 2) for i in parts]
            results = [
                local(phase * PAIRS + i, w[phase, pair].reshape(ITEMS, COLS)) for i, pair in zip(parts, pairs)
            ]
            for pair, result in zip(pairs, results):
                w[phase, pair] = result.reshape(2, ROWS, COLS)

        several(work)

    def arrived(chunks):
        for ch in chunks:
            pltpu.make_async_copy(vr.at[ch], vr.at[ch], vr_sem.at[ch]).wait()

    def grown(ch):
        values = vr[ch]
        high = values.astype(BF16).astype(F32)
        stack = jnp.concatenate([high, values - high, high, jnp.zeros((FAR, 2 * ITEMS), F32)], axis=0).astype(BF16)
        return turned_back(dot(stack, late[...], ((0,), (0,)))).reshape(2, ROWS, COLS)

    x = p // 8
    y = (p // 2) % 4
    core = p % 2
    parity = (x + y) % 2
    busy = polar & ((core == 0) | (parity == 0))
    mine = (2 * core + parity) * PAIRS + 2 * x + y // 2

    def v_copy(to):
        remote = pltpu.make_async_remote_copy(
            src_ref=vs.at[to], dst_ref=vr.at[mine], send_sem=v_sem, recv_sem=vr_sem.at[mine],
            device_id=(z, to), device_id_type=MESH,
        )
        return remote, pltpu.make_async_copy(vs.at[to], vr.at[mine], vr_sem.at[mine])

    @pl.when(polar)
    def _():
        several(
            lambda parts: shrink(
                [2 * PAIRS + i for i in parts],
                [th[pl.ds(2 * i, 2)].reshape(ITEMS, COLS) for i in parts],
            )
        )
        send_u(2)
        for side in range(2):
            near_copy(2, side).start()
        for k in range(5, 9):
            loads[k].wait()
        local_wind(0)

    @pl.when(busy)
    def _():
        pltpu.make_async_copy(zin, zin, z_sem).wait()
        high, low = split(zin[...].reshape(RING * FAR, 2 * ITEMS))
        result = (
            dot(cross[0], high, ((1,), (0,)))
            + dot(cross[0], low, ((1,), (0,)))
            + dot(cross[1], high, ((1,), (0,)))
        )
        vs[...] = result.reshape(RING, FAR, 2 * ITEMS)
        remote, own = v_copy(p)
        own.start()

        for i in range(1, RING):
            remote, own = v_copy((p + i) % RING)
            remote.start()

    @pl.when(polar)
    def _():
        for side in range(2):
            near_copy(2, side).wait()

        def local_thick(parts):
            pairs = [pl.ds(2 * i, 2) for i in parts]
            results = [local(2 * PAIRS + i, th[pair].reshape(ITEMS, COLS)) for i, pair in zip(parts, pairs)]
            for pair, result in zip(pairs, results):
                th[pair] = result.reshape(2, ROWS, COLS)

        several(local_thick)

        def work(parts):
            arrived([2 * PAIRS + i for i in parts])
            pairs = [pl.ds(2 * i, 2) for i in parts]
            results = [th[pair] + grown(2 * PAIRS + i) for i, pair in zip(parts, pairs)]
            for pair, result in zip(pairs, results):
                ext[pair, 0:ROWS, 0:COLS] = result

        several(work)

    @pl.when(jnp.logical_not(polar))
    def _():
        ext[:, 0:ROWS, 0:COLS] = th[...]

    def thick_first(i):
        return ext[2 * i : 2 * i + 2, 0:ROWS, 0:128].reshape(ITEMS, 128)[:, 0:1]

    def thick_last(i):
        return ext[2 * i : 2 * i + 2, 0:ROWS, 256:WIDE].reshape(ITEMS, 128)[:, COLS - 257 : COLS - 256]

    for side, row in ((0, ROWS - 1), (1, 0)):
        for lev in range(LEVELS):
            lat_out[1, side, lev : lev + 1, 0:COLS] = ext[lev, row : row + 1, 0:COLS]
        lat_copy(1, side, (1, BANDS - 1)[side]).start()
    send_lon(1, thick_first, thick_last)

    @pl.when(polar)
    def _():
        local_wind(1)
        for phase in range(2):

            def work(parts):
                arrived([phase * PAIRS + i for i in parts])
                pairs = [pl.ds(2 * i, 2) for i in parts]
                results = [w[phase, pair] + grown(phase * PAIRS + i) for i, pair in zip(parts, pairs)]
                for pair, result in zip(pairs, results):
                    w[phase, pair] = result

            several(work)

    wait_edges(1)
    for i in range(PAIRS):
        pair = slice(2 * i, 2 * i + 2)
        tile = ext[pair, 0:ROWS, 256:WIDE].reshape(ITEMS, 128)
        ext[pair, 0:ROWS, 256:WIDE] = with_edges(1, i, tile).reshape(2, ROWS, 128)
    for lev in range(LEVELS):
        ext[lev, ROWS : ROWS + 1] = jnp.where(z == BANDS - 1, 0.0, lat_in[1, 1, lev : lev + 1])
        ext[lev, ROWS + 7 : ROWS + 8] = jnp.where(z == 0, 0.0, lat_in[1, 0, lev : lev + 1])

    @pl.when(polar)
    def _():
        for phase in range(3):
            for t in range(PAIRS):
                to, remote, own = u_copy(phase, t)

                @pl.when(to != p)
                def _():
                    remote.wait_send()

    @pl.when(busy)
    def _():
        def step(i, carry):
            remote, own = v_copy((p + i) % RING)
            remote.wait_send()
            return carry

        lax.fori_loop(1, RING, step, 0)

    @pl.when(jnp.logical_not(polar))
    def _():
        for k in range(4, 9):
            loads[k].wait()


def gradient_kernel(ext_ref, wind_ref, thick_hbm, out_hbm, thick, out, done_sem):
    z, _ = place()
    slope = press_coef * latitude_tables(z)[1]
    copies = []
    for first in range(0, LEVELS, STEP):
        for lev in range(first, first + STEP):
            cells = ext_ref[lev]
            lon_diff = pltpu.roll(cells, WIDE - 1, 1) - pltpu.roll(cells, 1, 1)
            lat_diff = pltpu.roll(cells, ROWS + 7, 0) - pltpu.roll(cells, 1, 0)
            thick[lev] = cells[0:ROWS, 0:COLS]
            out[0, lev] = wind_ref[0, lev] - (slope * lon_diff[0:ROWS])[:, 0:COLS]
            out[1, lev] = wind_ref[1, lev] - (press_coef * lat_diff[0:ROWS])[:, 0:COLS]
        part = pl.ds(first, STEP)
        group = first // STEP
        copies += [
            pltpu.make_async_copy(thick.at[part], thick_hbm.at[part], done_sem.at[0, group]),
            pltpu.make_async_copy(out.at[0, part], out_hbm.at[0, part], done_sem.at[1, group]),
            pltpu.make_async_copy(out.at[1, part], out_hbm.at[1, part], done_sem.at[2, group]),
        ]
        for copy in copies[-3:]:
            copy.start()
    for copy in copies:
        copy.wait()


def body(thickness, wind, cutoff, tables):
    near, short, early, late, cross = tables
    any_space = pl.BlockSpec(memory_space=pl.ANY)
    dma = pltpu.SemaphoreType.DMA
    ext, moved = pl.pallas_call(
        far_kernel,
        out_shape=(
            pltpu.VMEM((LEVELS, ROWS + 8, WIDE), F32),
            pltpu.VMEM((2, LEVELS, ROWS, COLS), F32),
        ),
        in_specs=[pl.BlockSpec(memory_space=pltpu.HBM)] * 8,
        out_specs=(pl.BlockSpec(memory_space=pltpu.VMEM),) * 2,
        scratch_shapes=[
            pltpu.VMEM((1, 4 * ROWS), jnp.int32),
            pltpu.VMEM((LEVELS, ROWS, COLS), F32),
            pltpu.VMEM((CHUNKS, 2 * ITEMS, 2 * WIDE), BF16),
            pltpu.VMEM((3, ITEMS, WIDE), F32),
            pltpu.VMEM((2, ITEMS, WIDE), F32),
            pltpu.VMEM((4, ITEMS, WIDE), F32),
            pltpu.VMEM(near.shape, BF16),
            pltpu.VMEM(short.shape, BF16),
            pltpu.VMEM(early.shape, BF16),
            pltpu.VMEM(late.shape, BF16),
            pltpu.VMEM(cross.shape, BF16),
            pltpu.VMEM((CHUNKS, INNER, 2 * ITEMS), F32),
            pltpu.VMEM((2, CHUNKS, NEAR, 2 * ITEMS), F32),
            pltpu.VMEM((2, CHUNKS, NEAR, 2 * ITEMS), F32),
            pltpu.VMEM((CHUNKS, FAR, 2 * ITEMS), F32),
            pltpu.VMEM((RING, FAR, 2 * ITEMS), F32),
            pltpu.VMEM((RING, FAR, 2 * ITEMS), F32),
            pltpu.VMEM((CHUNKS, FAR, 2 * ITEMS), F32),
            pltpu.VMEM((2, ITEMS, 128), F32),
            pltpu.VMEM((2, 2, ITEMS, 128), F32),
            pltpu.VMEM((2, 2, LEVELS, WIDE), F32),
            pltpu.VMEM((2, 2, LEVELS, WIDE), F32),
            dma((9,)),
            dma((3, 2)),
            dma((3, 2)),
            dma,
            dma,
            dma,
            dma((CHUNKS,)),
            dma((2, 2)),
            dma((2, 2)),
            dma((2, 2)),
            dma((2, 2)),
        ],
        compiler_params=pltpu.CompilerParams(
            collective_id=0, has_side_effects=True, vmem_limit_bytes=61865984
        ),
        name="far",
    )(cutoff.reshape(1, -1), thickness, wind, near, short, early, late, cross)
    return pl.pallas_call(
        gradient_kernel,
        out_shape=(
            jax.ShapeDtypeStruct((LEVELS, ROWS, COLS), F32),
            jax.ShapeDtypeStruct((2, LEVELS, ROWS, COLS), F32),
        ),
        in_specs=[pl.BlockSpec(memory_space=pltpu.VMEM)] * 2,
        out_specs=(any_space, any_space),
        scratch_shapes=[
            pltpu.VMEM((LEVELS, ROWS, COLS), F32),
            pltpu.VMEM((2, LEVELS, ROWS, COLS), F32),
            dma((3, LEVELS // STEP)),
        ],
        compiler_params=pltpu.CompilerParams(vmem_limit_bytes=40 * 2**20),
        name="gradient",
    )(ext, moved)


def solution(mesh):
    tables = all_tables()
    in_specs = (P(None, "lat", "lon"), P(None, None, "lat", "lon"), P())
    out_specs = (P(None, "lat", "lon"), P(None, None, "lat", "lon"))

    def step(thickness, wind, cutoff):
        return body(thickness, wind, cutoff, tables)

    return jax.shard_map(step, mesh=mesh, in_specs=in_specs, out_specs=out_specs, check_vma=False)
```
